256 devices in a mesh: ang: 32 (over z_lo, x, core), gz: 8 (over z_hi, y).
Axes of the slice: x: 4, y: 4, z: 8 (z_hi: 2, z_lo: 4; z = z_hi * 4 + z_lo), core: 2. Of those that a mesh axis runs over, the one named last changes fastest.
Arguments:
- projections: bfloat16 [256, 512, 1024], P('ang', 'gz'), may hold values from -6 to 6
- band_weights: bfloat16 [256, 1024, 128], P('ang'), may hold values from -0.03125 to 0.03125
- band_offsets: int32 [256, 64], P('ang'), may hold values from 0 to 896
- phase: int32 [64, 512, 1024], P('ang', 'gz'), may hold values from 0 to 3
- contact: int32 [64, 512, 1024], P('ang', 'gz'), may hold values from 0 to 3
- conductivity_table: float32 [4, 4], replicated, may hold values from 0.1 to 1
Outputs:
- volume: float32 [64, 512, 1024], P('ang', 'gz')
- temperature: float32 [64, 512, 1024], P('ang', 'gz')
The draws below stay inside these ranges and needn't reach their ends.
Inputs may be any that keep to these rules, and one draw needn't show every extreme that they name: `band_offsets`: each band lies inside the detector.
All inputs are finite; a program needn't handle non-finite values.
Results may differ from the reference program's by a relative error of at most 0.0003.
Values sent between devices are 32-bit elements; how exact they have to be, the bound alone decides.
No kernel may reach another device: no remote copies, remote signals or barrier semaphores. Data moves between devices by JAX's collectives and lax.ppermute only.
A program may use at most 128 MiB of HBM per device.

```python
import math
import jax
import jax.numpy as jnp
from jax import lax

U = 1024
B = 128
NY = 1024
PHASES = 4
CONTACTS = 4
STEPS = 4
ANGLES = 256
NX = 64
NZ = 512


def with_ends(values, own_key, low, largest):
    place = [jax.random.randint(jax.random.fold_in(own_key, axis), (), 0, length) for axis, length in enumerate(values.shape)]
    main_axis = values.shape.index(max(values.shape))
    next_to = place[:main_axis] + [(place[main_axis] + 1) % values.shape[main_axis]] + place[main_axis + 1:]
    return values.at[tuple(place)].set(low).at[tuple(next_to)].set(largest)


def block_levels(key, dims, shards, least, top_value):
    factor_of = 1.0
    for axis_at, blocks in shards:
        steps = jax.random.uniform(jax.random.fold_in(jax.random.fold_in(key, 6), axis_at), (blocks,), jnp.float32, least / len(shards), top_value / len(shards))
        factor_of = factor_of * jnp.repeat(jnp.exp(steps), dims[axis_at] // blocks).reshape((-1,) + (1,) * (len(dims) - 1 - axis_at))
    return factor_of


def bell_draw(key, extent, width, most, cuts=(), held_as=jnp.bfloat16):
    drawn = jax.random.normal(key, extent, jnp.float32) * width
    if len(cuts) > 0:
        drawn = block_levels(key, extent, cuts, -0.22, 0.18) * drawn
    return jnp.clip(drawn, min=-most, max=most).astype(held_as)


def setup_inputs(seed: int = 0) -> dict:
    seeds = jax.random.split(jax.random.key(seed), 7)
    return {
        "projections": bell_draw(seeds[0], (ANGLES, NZ, U), 1.0, 6.0, ((0, 32), (1, 8))),
        "band_weights": bell_draw(seeds[1], (ANGLES, NY, B), (ANGLES * B) ** -0.5, 0.03125, ((0, 32),)),
        "band_offsets": with_ends(jax.random.randint(seeds[2], (ANGLES, NX), 0, U - B + 1), jax.random.fold_in(seeds[2], 1), 0, U - B).astype(jnp.int32),
        "phase": with_ends(jax.random.randint(seeds[3], (NX, NZ, NY), 0, PHASES), jax.random.fold_in(seeds[3], 1), 0, PHASES - 1).astype(jnp.int32),
        "contact": with_ends(jax.random.randint(seeds[4], (NX, NZ, NY), 0, CONTACTS), jax.random.fold_in(seeds[4], 1), 0, CONTACTS - 1).astype(jnp.int32),
        "conductivity_table": jnp.clip(jnp.exp(jax.random.uniform(seeds[5], (PHASES, CONTACTS), jnp.float32, math.log(0.1), math.log(1.0))), 0.1, 1.0),
    }


step_size = 0.15


def advance(heat_wide, conduct_wide):
    heat_pad = jnp.pad(heat_wide, ((0, 0), (0, 0), (1, 1)))
    conduct_pad = jnp.pad(conduct_wide, ((0, 0), (0, 0), (1, 1)))
    centre = heat_pad[1:-1, 1:-1, 1:-1]
    conduct_mid = conduct_pad[1:-1, 1:-1, 1:-1]
    pieces = [
        (heat_pad[2:, 1:-1, 1:-1], conduct_pad[2:, 1:-1, 1:-1]),
        (heat_pad[:-2, 1:-1, 1:-1], conduct_pad[:-2, 1:-1, 1:-1]),
        (heat_pad[1:-1, 1:-1, 2:], conduct_pad[1:-1, 1:-1, 2:]),
        (heat_pad[1:-1, 1:-1, :-2], conduct_pad[1:-1, 1:-1, :-2]),
        (heat_pad[1:-1, 2:, 1:-1], conduct_pad[1:-1, 2:, 1:-1]),
        (heat_pad[1:-1, :-2, 1:-1], conduct_pad[1:-1, :-2, 1:-1]),
    ]
    flux_sum = jnp.zeros_like(centre)
    for heat_near, conduct_near in pieces:
        denominator = conduct_mid + conduct_near
        positive = denominator > 0.0
        safe_denominator = jnp.where(positive, denominator, 1.0)
        face = jnp.where(positive, 2.0 * conduct_mid * conduct_near / safe_denominator, 0.0)
        flux_sum = flux_sum + face * (heat_near - centre)
    return centre + step_size * flux_sum


def reference(projections, band_weights, band_offsets, phase, contact, conductivity_table):
    angle_ids = jnp.arange(ANGLES, dtype=jnp.int32)[:, None, None]
    depth_ids = jnp.arange(NZ, dtype=jnp.int32)[None, :, None]
    spread = jnp.arange(B, dtype=jnp.int32)[None, :]
    weights_wide = band_weights.astype(jnp.float32)

    def one_row(offsets_row):
        columns = (offsets_row[:, None] + spread).astype(jnp.int32)
        gathered = projections[angle_ids, depth_ids, columns[:, None, :]].astype(jnp.float32)
        return jnp.einsum('ayb,azb->zy', weights_wide, gathered, precision=lax.Precision.HIGHEST)

    volume = lax.map(one_row, band_offsets.T)
    conduct = conductivity_table[phase, contact].astype(jnp.float32)
    conduct_wide = jnp.pad(conduct, ((1, 1), (1, 1), (0, 0)))
    heat_field = volume
    for section in range(STEPS):
        heat_field = advance(jnp.pad(heat_field, ((1, 1), (1, 1), (0, 0))), conduct_wide)
    return volume, heat_field
```

```python
import functools
import jax
import jax.numpy as jnp
from jax import lax
from jax.experimental import pallas as pl
from jax.experimental.pallas import tpu as pltpu
from jax.sharding import PartitionSpec as P

STEPS = 4
STEP_SIZE = 0.15
CHUNKS = 4
ZL, X, C = 4, 4, 2
VMEM_LIMIT = 56 * 1024 * 1024


def shift_ang(value, dz=0, dx=0, dc=0):
    perm = []
    for z in range(ZL):
        for x in range(X):
            for c in range(C):
                src = (z * X + x) * C + c
                dst = (((z + dz) % ZL) * X + (x + dx) % X) * C + (c ^ dc)
                perm.append((src, dst))
    return lax.ppermute(value, "ang", perm)


def shift_line(value, axis, step):
    count = lax.axis_size(axis)
    perm = [(i, i + step) for i in range(count) if 0 <= i + step < count]
    return lax.ppermute(value, axis, perm)


def gather_and_multiply(pos, offsets, proj, weights, wide, bands, core, store):
    angles, depth, columns = proj.shape
    wide[:, :, columns:] = jnp.zeros((angles, depth, 128), jnp.float32)
    for a in range(angles):
        wide[a, :, :columns] = proj[a].astype(jnp.float32)
    lane = lax.broadcasted_iota(jnp.int32, (depth, 128), 1)

    def row_body(row, carry):
        dx, dz, i = row // 8, (row // 2) % 4, row % 2
        owner = (
            ((pos[0] + dz) % ZL) * (X * C * 2) + ((pos[1] + dx) % X) * (C * 2) + core * 2 + i
        )
        for a in range(angles):
            off = offsets[a, owner]
            base = pl.multiple_of((off // 128) * 128, 128)
            rem = off % 128
            low = wide[a, :, pl.ds(base, 128)]
            high = wide[a, :, pl.ds(pl.multiple_of(base + 128, 128), 128)]
            turn = (128 - rem) % 128
            low = pltpu.roll(low, turn, 1)
            high = pltpu.roll(high, turn, 1)
            band = jnp.where(lane < 128 - rem, low, high)
            bands[pl.ds(pl.multiple_of(row * depth, depth), depth), a * 128:(a + 1) * 128] = (
                band.astype(jnp.bfloat16)
            )
        return carry

    lax.fori_loop(0, bands.shape[0] // depth, row_body, 0)
    tile = 256

    def tile_body(n, carry):
        cols = pl.ds(pl.multiple_of(n * tile, tile), tile)
        out = jnp.dot(bands[...], weights[:, cols], preferred_element_type=jnp.float32)
        store(out.reshape(4, 4, 2, depth, tile), cols)
        return carry

    lax.fori_loop(0, weights.shape[1] // tile, tile_body, 0)


def other_kernel(pos, offsets, proj, weights, out, wide, bands):
    def store(value, cols):
        out[:, :, :, :, cols] = value

    gather_and_multiply(pos, offsets, proj, weights, wide, bands, 1 - pos[2], store)


def mine_kernel(pos, offsets, proj, weights, recv, sendp, sendm, holdp, holdm, home, wide, bands):
    def store(value, cols):
        value = value + recv[:, :, :, :, cols]
        sendp[:2, :, :, cols] = value[2, :2]
        sendp[2:, :, :, cols] = value[1, 2:]
        sendm[:2, :, :, cols] = value[2, 2:]
        sendm[2:, :, :, cols] = value[3, :2]
        holdp[:, :, :, cols] = value[1, :2]
        holdm[:, :, :, cols] = value[3, 2:]
        home[:, :, :, cols] = value[0]

    gather_and_multiply(pos, offsets, proj, weights, wide, bands, pos[2], store)


SMEM = pl.BlockSpec(memory_space=pltpu.SMEM)
VMEM = pl.BlockSpec(memory_space=pltpu.VMEM)


def backproject(pos, offsets, proj, weights, chunk, recv=None):
    angles, depth_all, columns = proj.shape
    depth = depth_all // CHUNKS
    wide_y = weights.shape[1]
    proj_spec = pl.BlockSpec((angles, depth, columns), lambda i: (0, chunk, 0))
    full = lambda shape: pl.BlockSpec(shape, lambda i: (0,) * len(shape))
    scratch = [
        pltpu.VMEM((angles, depth, columns + 128), jnp.float32),
        pltpu.VMEM((32 * depth, angles * 128), jnp.bfloat16),
    ]
    flops = 2 * 32 * depth * angles * 128 * wide_y
    params = dict(
        scratch_shapes=scratch,
        grid=(1,),
        compiler_params=pltpu.CompilerParams(vmem_limit_bytes=VMEM_LIMIT),
        cost_estimate=pl.CostEstimate(flops=flops, bytes_accessed=6 * 2**20, transcendentals=0),
    )
    specs = [SMEM, SMEM, proj_spec, full(weights.shape)]
    f32 = lambda *shape: jax.ShapeDtypeStruct(shape, jnp.float32)
    if recv is None:
        shape = (4, 4, 2, depth, wide_y)
        return pl.pallas_call(
            other_kernel, out_shape=f32(*shape), in_specs=specs, out_specs=full(shape), **params
        )(pos, offsets, proj, weights)
    shapes = [(n, 2, depth, wide_y) for n in (4, 4, 2, 2, 4)]
    return pl.pallas_call(
        mine_kernel,
        out_shape=[f32(*s) for s in shapes],
        in_specs=specs + [full(recv.shape)],
        out_specs=[full(s) for s in shapes],
        **params,
    )(pos, offsets, proj, weights, recv)


def conduct_kernel(table, phase, contact, out):
    contacts = table.shape[1]
    index = phase[...] * contacts + contact[...]
    value = jnp.zeros(index.shape, jnp.float32)
    for p in range(table.shape[0]):
        for c in range(contacts):
            value = jnp.where(index == p * contacts + c, table[p, c], value)
    out[...] = value


def conductivities(table, phase, contact):
    rows = phase.shape[1]
    spec = pl.BlockSpec((1, 16, phase.shape[2]), lambda i, j: (i, j, 0))
    return pl.pallas_call(
        conduct_kernel,
        grid=(phase.shape[0], rows // 16),
        out_shape=jax.ShapeDtypeStruct(phase.shape, jnp.float32),
        in_specs=[SMEM, spec, spec],
        out_specs=spec,
    )(table, phase, contact)


def widened(value):
    below = [shift_line(value, "ang", 2), shift_line(value, "ang", 1)]
    above = [shift_line(value, "ang", -1), shift_line(value, "ang", -2)]
    wide = jnp.concatenate([*below, value, *above], axis=0)
    low = shift_line(wide[:, -4:], "gz", 1)
    high = shift_line(wide[:, :4], "gz", -1)
    return wide, low, high


def face_of(a, b):
    total = a + b
    positive = total > 0.0
    return jnp.where(positive, 2.0 * a * b / jnp.where(positive, total, 1.0), 0.0)


def heat_kernel(heat, heat_low, heat_high, cond, cond_low, cond_high, out, field, other, con, fx, fy, fz):
    rows, depth, columns = heat.shape
    tall = depth + 16
    for scratch, value, low, high in (
        (field, heat, heat_low, heat_high),
        (con, cond, cond_low, cond_high),
    ):
        zeros = jnp.zeros((rows, 8, columns), jnp.float32)
        scratch[:, :8] = zeros
        scratch[:, depth + 8:] = zeros
        scratch[:, 4:8] = low[...]
        scratch[:, depth + 8:depth + 12] = high[...]
        scratch[:, 8:depth + 8] = value[...]
    tiles = tall // 8
    lane = lax.broadcasted_iota(jnp.int32, (8, columns), 1)
    sub = lax.broadcasted_iota(jnp.int32, (8, columns), 0)

    def next_z(here, above):
        return jnp.where(sub == 7, pltpu.roll(above, 7, 0), pltpu.roll(here, 7, 0))

    def face_body(r, carry):
        here = con[r, 0:8, :]
        for t in range(tiles):
            z = slice(8 * t, 8 * t + 8)
            above = con[r, 8 * t + 8:8 * t + 16, :] if t + 1 < tiles else jnp.zeros_like(here)
            along_y = pltpu.roll(here, columns - 1, 1)
            fy[r, z, :] = jnp.where(lane == columns - 1, 0.0, face_of(here, along_y))
            fz[r, z, :] = face_of(here, next_z(here, above))
            fx[r, z, :] = face_of(here, con[jnp.minimum(r + 1, rows - 1), z, :])
            here = above
        return carry

    lax.fori_loop(0, rows, face_body, 0)

    source, target = field, other
    for step in range(1, STEPS + 1):
        last = step == STEPS
        first_tile, end_tile = (1, tiles - 1) if last else (0, tiles)

        def row_body(r, carry, source=source, target=target, last=last, first_tile=first_tile, end_tile=end_tile):
            if first_tile:
                before = source[r, 8 * first_tile - 8:8 * first_tile, :]
                here = source[r, 8 * first_tile:8 * first_tile + 8, :]
                flux_before = fz[r, 8 * first_tile - 8:8 * first_tile, :] * (
                    next_z(before, here) - before
                )
            else:
                here = source[r, 0:8, :]
                flux_before = jnp.zeros_like(here)
            for t in range(first_tile, end_tile):
                z = slice(8 * t, 8 * t + 8)
                above = source[r, 8 * t + 8:8 * t + 16, :] if t + 1 < tiles else jnp.zeros_like(here)
                flux_x = fx[r, z, :] * (source[r + 1, z, :] - here)
                flux_x -= fx[r - 1, z, :] * (here - source[r - 1, z, :])
                flux_y = fy[r, z, :] * (pltpu.roll(here, columns - 1, 1) - here)
                flux_y -= pltpu.roll(flux_y, 1, 1)
                flux = fz[r, z, :] * (next_z(here, above) - here)
                flux_z = flux - jnp.where(sub == 0, pltpu.roll(flux_before, 1, 0), pltpu.roll(flux, 1, 0))
                value = here + STEP_SIZE * (flux_x + flux_y + flux_z)
                if last:
                    out[r - STEPS, 8 * t - 8:8 * t, :] = value
                else:
                    target[r, z, :] = value
                here, flux_before = above, flux
            return carry

        lax.fori_loop(step, rows - step, row_body, 0)
        source, target = target, source


def conduct_heat(heat, cond):
    rows, depth, columns = heat[0].shape
    scratch = pltpu.VMEM((rows, depth + 16, columns), jnp.float32)
    return pl.pallas_call(
        heat_kernel,
        out_shape=jax.ShapeDtypeStruct((rows - 2 * STEPS, depth, columns), jnp.float32),
        in_specs=[VMEM] * 6,
        out_specs=VMEM,
        scratch_shapes=[scratch] * 6,
        compiler_params=pltpu.CompilerParams(vmem_limit_bytes=VMEM_LIMIT),
        cost_estimate=pl.CostEstimate(
            flops=200 * 2**20, bytes_accessed=6 * 2**20, transcendentals=0
        ),
    )(*heat, *cond)


def local(projections, band_weights, band_offsets, phase, contact, conductivity_table):
    angles, wide_y, band = band_weights.shape
    ang = lax.axis_index("ang")
    pos = jnp.stack([ang // (X * C), (ang // C) % X, ang % C]).astype(jnp.int32)
    weights = jnp.transpose(band_weights, (0, 2, 1)).reshape(angles * band, wide_y)
    conduct = conductivities(conductivity_table, phase, contact)
    conduct_wide = widened(conduct)

    pieces = []
    for chunk in range(CHUNKS):
        theirs = backproject(pos, band_offsets, projections, weights, chunk)
        recv = shift_ang(theirs, dc=1)
        sendp, sendm, holdp, holdm, home = backproject(
            pos, band_offsets, projections, weights, chunk, recv
        )
        fromp = shift_ang(sendp, dx=1)
        fromm = shift_ang(sendm, dx=-1)
        lastp = shift_ang(holdp + fromp[:2], dx=1)
        lastm = shift_ang(holdm + fromm[:2], dx=-1)
        ring_low = home[:2] + lastp + fromm[2:]
        ring_high = home[2:] + lastm + fromp[2:]
        one = shift_ang(ring_low[1], dz=1)
        two = shift_ang(ring_high[0], dz=2)
        three = shift_ang(ring_high[1], dz=3)
        pieces.append(ring_low[0] + one + two + three)
    volume = jnp.concatenate(pieces, axis=1)
    temperature = conduct_heat(widened(volume), conduct_wide)
    return volume, temperature


def solution(mesh):
    in_specs = (
        P("ang", "gz", None),
        P("ang", None, None),
        P("ang", None),
        P("ang", "gz", None),
        P("ang", "gz", None),
        P(),
    )
    out_specs = (P("ang", "gz", None), P("ang", "gz", None))
    return jax.shard_map(local, mesh=mesh, in_specs=in_specs, out_specs=out_specs, check_vma=False)
```

```python
import functools
import jax
import jax.numpy as jnp
from jax import lax
from jax.experimental import pallas as pl
from jax.experimental.pallas import tpu as pltpu
from jax.sharding import PartitionSpec as P

STEPS = 4
STEP_SIZE = 0.15
CHUNKS = ((0, 16), (32, 32), (16, 16))
ZL, X, C = 4, 4, 2
VMEM_LIMIT = 26 * 1024 * 1024


def shift_ang(value, dz=0, dx=0, dc=0):
    perm = []
    for z in range(ZL):
        for x in range(X):
            for c in range(C):
                src = (z * X + x) * C + c
                dst = (((z + dz) % ZL) * X + (x + dx) % X) * C + (c ^ dc)
                perm.append((src, dst))
    return lax.ppermute(value, "ang", perm)


def shift_line(value, axis, step):
    count = lax.axis_size(axis)
    perm = [(i, i + step) for i in range(count) if 0 <= i + step < count]
    return lax.ppermute(value, axis, perm)


def gather_and_multiply(pos, offsets, proj, weights, wide, bands, flat, sems, core, store):
    angles, depth, columns = proj.shape
    copies = [
        pltpu.make_async_copy(weights.at[a], flat.at[:, a * 128:(a + 1) * 128], sems.at[a])
        for a in range(angles)
    ]
    for copy in copies:
        copy.start()
    wide[:, :, columns:] = jnp.zeros((angles, depth, 128), jnp.float32)
    for a in range(angles):
        wide[a, :, :columns] = proj[a].astype(jnp.float32)
    lane = lax.broadcasted_iota(jnp.int32, (depth, 128), 1)

    def row_body(row, carry):
        dx, dz, i = row >> 3, (row >> 1) & 3, row & 1
        owner = (
            ((pos[0] + dz) & (ZL - 1)) * (X * C * 2)
            + ((pos[1] + dx) & (X - 1)) * (C * 2)
            + core * 2
            + i
        )
        for a in range(angles):
            off = offsets[a, owner]
            base = pl.multiple_of((off >> 7) << 7, 128)
            rem = off & 127
            low = wide[a, :, pl.ds(base, 128)]
            high = wide[a, :, pl.ds(pl.multiple_of(base + 128, 128), 128)]
            band = pltpu.roll(jnp.where(lane < rem, high, low), (128 - rem) & 127, 1)
            bands[pl.ds(pl.multiple_of(row * depth, depth), depth), a * 128:(a + 1) * 128] = (
                band.astype(jnp.bfloat16)
            )
        return carry

    lax.fori_loop(0, bands.shape[0] // depth, row_body, 0, unroll=4)
    for copy in copies:
        copy.wait()
    tile = 256
    for n in range(0, flat.shape[0], tile):
        out = lax.dot_general(
            bands[...],
            flat[n:n + tile, :],
            (((1,), (1,)), ((), ())),
            preferred_element_type=jnp.float32,
        )
        store(out.reshape(4, 4, 2, depth, tile), slice(n, n + tile))


def other_kernel(pos, offsets, proj, weights, out, *scratch):
    def store(value, cols):
        out[:, :, :, :, cols] = value

    gather_and_multiply(pos, offsets, proj, weights, *scratch, 1 - pos[2], store)


def mine_kernel(pos, offsets, proj, weights, recv, sendp, sendm, holdp, holdm, home, *scratch):
    def store(value, cols):
        value = value + recv[:, :, :, :, cols]
        sendp[:2, :, :, cols] = value[2, :2]
        sendp[2:, :, :, cols] = value[1, 2:]
        sendm[:2, :, :, cols] = value[2, 2:]
        sendm[2:, :, :, cols] = value[3, :2]
        holdp[:, :, :, cols] = value[1, :2]
        holdm[:, :, :, cols] = value[3, 2:]
        home[:, :, :, cols] = value[0]

    gather_and_multiply(pos, offsets, proj, weights, *scratch, pos[2], store)


SMEM = pl.BlockSpec(memory_space=pltpu.SMEM)
VMEM = pl.BlockSpec(memory_space=pltpu.VMEM)
ANY = pl.BlockSpec(memory_space=pl.ANY)


def cost(us):
    return pl.CostEstimate(flops=int(us * 1.1e9), bytes_accessed=2**20, transcendentals=0)


def backproject(pos, offsets, proj, weights, start, depth, recv=None):
    angles, _, columns = proj.shape
    wide_y, band = weights.shape[1:]
    full = lambda shape: pl.BlockSpec(shape, lambda i: (0,) * len(shape))
    params = dict(
        scratch_shapes=[
            pltpu.VMEM((angles, depth, columns + 128), jnp.float32),
            pltpu.VMEM((32 * depth, angles * band), jnp.bfloat16),
            pltpu.VMEM((wide_y, angles * band), jnp.bfloat16),
            pltpu.SemaphoreType.DMA((angles,)),
        ],
        grid=(1,),
        compiler_params=pltpu.CompilerParams(vmem_limit_bytes=VMEM_LIMIT),
        cost_estimate=cost(4.0 if depth == 16 else 6.0),
    )
    proj_spec = pl.BlockSpec((angles, depth, columns), lambda i: (0, start // depth, 0))
    specs = [SMEM, SMEM, proj_spec, ANY]
    f32 = lambda *shape: jax.ShapeDtypeStruct(shape, jnp.float32)
    if recv is None:
        shape = (4, 4, 2, depth, wide_y)
        return pl.pallas_call(
            other_kernel, out_shape=f32(*shape), in_specs=specs, out_specs=full(shape), **params
        )(pos, offsets, proj, weights)
    shapes = [(n, 2, depth, wide_y) for n in (4, 4, 2, 2, 4)]
    return pl.pallas_call(
        mine_kernel,
        out_shape=[f32(*s) for s in shapes],
        in_specs=specs + [full(recv.shape)],
        out_specs=[full(s) for s in shapes],
        **params,
    )(pos, offsets, proj, weights, recv)


def conduct_kernel(table, phase, contact, out):
    for r in range(phase.shape[0]):
        for z in range(0, phase.shape[1], 8):
            label = phase[r, z:z + 8, :]
            other = contact[r, z:z + 8, :]
            odd, upper = (other & 1) == 1, other >= 2
            odd_row, upper_row = (label & 1) == 1, label >= 2
            rows = [
                jnp.where(
                    upper,
                    jnp.where(odd, table[p, 3], table[p, 2]),
                    jnp.where(odd, table[p, 1], table[p, 0]),
                )
                for p in range(4)
            ]
            out[r, z:z + 8, :] = jnp.where(
                upper_row,
                jnp.where(odd_row, rows[3], rows[2]),
                jnp.where(odd_row, rows[1], rows[0]),
            )


def conductivities(table, phase, contact):
    return pl.pallas_call(
        conduct_kernel,
        out_shape=jax.ShapeDtypeStruct(phase.shape, jnp.float32),
        in_specs=[SMEM, VMEM, VMEM],
        out_specs=VMEM,
        cost_estimate=cost(2.0),
    )(table, phase, contact)


def widened(core, value):
    left = shift_line(value, "ang", 2)
    right = shift_line(value, "ang", -2)
    first = core == 0
    given = jnp.concatenate([jnp.where(first, value, left), jnp.where(first, right, value)], axis=0)
    got = shift_ang(given, dc=1)
    return [left, got, value, right]


def ends(pieces_low, pieces_high):
    def rows(pieces, z):
        left, got, value, right = (p[:, z] for p in pieces)
        return jnp.concatenate([left, got[:2], value, got[2:], right], axis=0)

    low = shift_line(rows(pieces_high, slice(-4, None)), "gz", 1)
    high = shift_line(rows(pieces_low, slice(0, 4)), "gz", -1)
    return low, high


def fill(scratch, groups, low, high):
    rows, tall, columns = scratch.shape
    zeros = jnp.zeros((rows, 8, columns), jnp.float32)
    scratch[:, :8] = zeros
    scratch[:, tall - 8:] = zeros
    scratch[:, 4:8] = low[...]
    scratch[:, tall - 8:tall - 4] = high[...]
    for start, (left, got, value, right) in groups:
        z = slice(8 + start, 8 + start + value.shape[1])
        scratch[0:2, z] = left[...]
        scratch[2:4, z] = got[:2]
        scratch[4:6, z] = value[...]
        scratch[6:8, z] = got[2:]
        scratch[8:10, z] = right[...]


def face_of(a, b):
    total = a + b
    positive = total > 0.0
    return jnp.where(positive, 2.0 * a * b / jnp.where(positive, total, 1.0), 0.0)


def next_z(sub, here, above):
    return jnp.where(sub == 7, pltpu.roll(above, 7, 0), pltpu.roll(here, 7, 0))


def faces_kernel(left, got, value, right, low, high, fx, fy, fz, con):
    fill(con, [(0, (left, got, value, right))], low, high)
    rows, tall, columns = con.shape
    tiles = tall // 8
    lane = lax.broadcasted_iota(jnp.int32, (8, columns), 1)
    sub = lax.broadcasted_iota(jnp.int32, (8, columns), 0)

    def face_body(r, carry):
        here = con[r, 0:8, :]
        for t in range(tiles):
            z = slice(8 * t, 8 * t + 8)
            above = con[r, 8 * t + 8:8 * t + 16, :] if t + 1 < tiles else jnp.zeros_like(here)
            along_y = pltpu.roll(here, columns - 1, 1)
            fy[r, z, :] = jnp.where(lane == columns - 1, 0.0, face_of(here, along_y))
            fz[r, z, :] = face_of(here, next_z(sub, here, above))
            fx[r, z, :] = face_of(here, con[jnp.minimum(r + 1, rows - 1), z, :])
            here = above
        return carry

    lax.fori_loop(0, rows, face_body, 0)


def faces(cond, low, high):
    _, depth, columns = cond[2].shape
    shape = (2 * STEPS + 2, depth + 16, columns)
    return pl.pallas_call(
        faces_kernel,
        out_shape=[jax.ShapeDtypeStruct(shape, jnp.float32)] * 3,
        in_specs=[VMEM] * 6,
        out_specs=[VMEM] * 3,
        scratch_shapes=[pltpu.VMEM(shape, jnp.float32)],
        compiler_params=pltpu.CompilerParams(vmem_limit_bytes=VMEM_LIMIT),
        cost_estimate=cost(6.0),
    )(*cond, low, high)


def heat_kernel(starts, *refs):
    count = 4 * len(starts)
    parts, (low, high, fx, fy, fz, out, field, other) = refs[:count], refs[count:]
    fill(field, [(s, parts[4 * n:4 * n + 4]) for n, s in enumerate(starts)], low, high)
    rows, tall, columns = field.shape
    tiles = tall // 8
    sub = lax.broadcasted_iota(jnp.int32, (8, columns), 0)
    source, target = field, other
    for step in range(1, STEPS + 1):
        last = step == STEPS
        first_tile, end_tile = (1, tiles - 1) if last else (0, tiles)

        def row_body(r, carry, source=source, target=target, last=last, first_tile=first_tile, end_tile=end_tile):
            if first_tile:
                before = source[r, 8 * first_tile - 8:8 * first_tile, :]
                here = source[r, 8 * first_tile:8 * first_tile + 8, :]
                flux_before = fz[r, 8 * first_tile - 8:8 * first_tile, :] * (
                    next_z(sub, before, here) - before
                )
            else:
                here = source[r, 0:8, :]
                flux_before = jnp.zeros_like(here)
            for t in range(first_tile, end_tile):
                z = slice(8 * t, 8 * t + 8)
                above = source[r, 8 * t + 8:8 * t + 16, :] if t + 1 < tiles else jnp.zeros_like(here)
                flux_x = fx[r, z, :] * (source[r + 1, z, :] - here)
                flux_x -= fx[r - 1, z, :] * (here - source[r - 1, z, :])
                flux_y = fy[r, z, :] * (pltpu.roll(here, columns - 1, 1) - here)
                flux_y -= pltpu.roll(flux_y, 1, 1)
                flux = fz[r, z, :] * (next_z(sub, here, above) - here)
                flux_z = flux - jnp.where(sub == 0, pltpu.roll(flux_before, 1, 0), pltpu.roll(flux, 1, 0))
                value = here + STEP_SIZE * (flux_x + flux_y + flux_z)
                if last:
                    out[r - STEPS, 8 * t - 8:8 * t, :] = value
                else:
                    target[r, z, :] = value
                here, flux_before = above, flux
            return carry

        lax.fori_loop(step, rows - step, row_body, 0)
        source, target = target, source


def conduct_heat(groups, low, high, face_arrays):
    rows, tall, columns = face_arrays[0].shape
    parts = [p for _, group in groups for p in group]
    return pl.pallas_call(
        functools.partial(heat_kernel, [s for s, _ in groups]),
        out_shape=jax.ShapeDtypeStruct((rows - 2 * STEPS, tall - 16, columns), jnp.float32),
        in_specs=[VMEM] * (len(parts) + 5),
        out_specs=VMEM,
        scratch_shapes=[pltpu.VMEM((rows, tall, columns), jnp.float32)] * 2,
        compiler_params=pltpu.CompilerParams(vmem_limit_bytes=VMEM_LIMIT),
        cost_estimate=cost(9.0),
    )(*parts, low, high, *face_arrays)


def reduced(pos, offsets, proj, weights, start, depth):
    theirs = backproject(pos, offsets, proj, weights, start, depth)
    recv = shift_ang(theirs, dc=1)
    sendp, sendm, holdp, holdm, home = backproject(pos, offsets, proj, weights, start, depth, recv)
    fromp = shift_ang(sendp, dx=1)
    fromm = shift_ang(sendm, dx=-1)
    lastp = shift_ang(holdp + fromp[:2], dx=1)
    lastm = shift_ang(holdm + fromm[:2], dx=-1)
    ring_low = home[:2] + lastp + fromm[2:]
    ring_high = home[2:] + lastm + fromp[2:]
    one = shift_ang(ring_low[1], dz=1)
    two = shift_ang(ring_high[0], dz=2)
    three = shift_ang(ring_high[1], dz=3)
    return ring_low[0] + one + two + three


def local(projections, band_weights, band_offsets, phase, contact, conductivity_table):
    ang = lax.axis_index("ang")
    core = ang & 1
    pos = jnp.stack([ang >> 3, (ang >> 1) & 3, core]).astype(jnp.int32)
    conduct = conductivities(conductivity_table, phase, contact)
    cond = widened(core, conduct)
    face_arrays = faces(cond, *ends(cond, cond))
    args = (pos, band_offsets, projections, band_weights)
    volumes = [reduced(*args, start, depth) for start, depth in CHUNKS]
    groups = [(start, widened(core, v)) for (start, _), v in zip(CHUNKS, volumes)]
    lowest = min(groups, key=lambda g: g[0])[1]
    highest = max(groups, key=lambda g: g[0])[1]
    temperature = conduct_heat(groups, *ends(lowest, highest), face_arrays)
    ordered = sorted(zip((s for s, _ in CHUNKS), volumes), key=lambda g: g[0])
    return jnp.concatenate([v for _, v in ordered], axis=1), temperature


def solution(mesh):
    in_specs = (
        P("ang", "gz", None),
        P("ang", None, None),
        P("ang", None),
        P("ang", "gz", None),
        P("ang", "gz", None),
        P(),
    )
    out_specs = (P("ang", "gz", None), P("ang", "gz", None))
    return jax.shard_map(local, mesh=mesh, in_specs=in_specs, out_specs=out_specs, check_vma=False)
```

```python
import functools
import jax
import jax.numpy as jnp
from jax import lax
from jax.experimental import pallas as pl
from jax.experimental.pallas import tpu as pltpu
from jax.sharding import PartitionSpec as P

STEPS = 4
STEP_SIZE = 0.15
CHUNKS = (((0, 16), (48, 16)), ((16, 32),))
TILE = 256
NEAR_US = 9.0
SWAP_US = 14.0
ZL, X, C = 4, 4, 2
VMEM_LIMIT = 26 * 1024 * 1024


def shift_ang(value, dz=0, dx=0, dc=0):
    perm = []
    for z in range(ZL):
        for x in range(X):
            for c in range(C):
                src = (z * X + x) * C + c
                dst = ((z ^ dz) * X + (x + dx) % X) * C + (c ^ dc)
                perm.append((src, dst))
    return lax.ppermute(value, "ang", perm)


def shift_line(value, axis, step):
    count = lax.axis_size(axis)
    perm = [(i, i + step) for i in range(count) if 0 <= i + step < count]
    return lax.ppermute(value, axis, perm)


def gather(ranges, pos, offsets, proj, weights, wide, bands, flat, sems, core):
    angles, _, columns = proj.shape
    depth = wide.shape[1]
    copies = [
        pltpu.make_async_copy(weights.at[a], flat.at[:, a * 128:(a + 1) * 128], sems.at[a])
        for a in range(angles)
    ]
    for copy in copies:
        copy.start()
    wide[:, :, columns:] = jnp.zeros((angles, depth, 128), jnp.float32)
    for a in range(angles):
        at = 0
        for first, count in ranges:
            wide[a, at:at + count, :columns] = proj[a, first:first + count, :].astype(jnp.float32)
            at += count
    lane = lax.broadcasted_iota(jnp.int32, (depth, 128), 1)

    def row_body(row, carry):
        dx, dz, i = row >> 3, (row >> 1) & 3, row & 1
        owner = (
            (pos[0] ^ dz) * (X * C * 2)
            + ((pos[1] + dx) & (X - 1)) * (C * 2)
            + core * 2
            + i
        )
        for a in range(angles):
            off = offsets[a, owner]
            base = pl.multiple_of((off >> 7) << 7, 128)
            rem = off & 127
            low = wide[a, :, pl.ds(base, 128)]
            high = wide[a, :, pl.ds(pl.multiple_of(base + 128, 128), 128)]
            band = pltpu.roll(jnp.where(lane < rem, high, low), (128 - rem) & 127, 1)
            bands[pl.ds(pl.multiple_of(row * depth, depth), depth), a * 128:(a + 1) * 128] = (
                band.astype(jnp.bfloat16)
            )
        return carry

    lax.fori_loop(0, bands.shape[0] // depth, row_body, 0, unroll=4)
    for copy in copies:
        copy.wait()


def product(bands, flat, store):
    for n in range(0, flat.shape[0], TILE):
        out = lax.dot_general(
            bands[...],
            flat[n:n + TILE, :],
            (((1,), (1,)), ((), ())),
            preferred_element_type=jnp.float32,
        )
        store(out.reshape(4, 4, 2, bands.shape[0] // 32, TILE), slice(n, n + TILE))


def other_kernel(ranges, pos, offsets, proj, weights, token, out, wide, bands, flat, sems):
    def store(value, cols):
        out[:, :, :, :, cols] = value

    gather(ranges, pos, offsets, proj, weights, wide, bands, flat, sems, 1 - pos[2])
    product(bands, flat, store)


def mine_kernel(
    ranges,
    pos,
    offsets,
    proj,
    weights,
    token,
    recv,
    sendp,
    sendm,
    holdp,
    holdm,
    home,
    wide,
    bands,
    flat,
    sems,
):
    def store(value, cols):
        value = value + recv[:, :, :, :, cols]
        sendp[:2, :, :, cols] = value[2, :2]
        sendp[2:, :, :, cols] = value[1, 2:]
        sendm[:2, :, :, cols] = value[2, 2:]
        sendm[2:, :, :, cols] = value[3, :2]
        holdp[:, :, :, cols] = value[1, :2]
        holdm[:, :, :, cols] = value[3, 2:]
        home[:, :, :, cols] = value[0]

    gather(ranges, pos, offsets, proj, weights, wide, bands, flat, sems, pos[2])
    product(bands, flat, store)


SMEM = pl.BlockSpec(memory_space=pltpu.SMEM)
VMEM = pl.BlockSpec(memory_space=pltpu.VMEM)
ANY = pl.BlockSpec(memory_space=pl.ANY)


def cost(us):
    return pl.CostEstimate(flops=int(us * 1.1e9), bytes_accessed=2**20, transcendentals=0)


def backproject(pos, offsets, proj, weights, ranges, token, recv=None):
    angles, _, columns = proj.shape
    wide_y, band = weights.shape[1:]
    depth = sum(count for _, count in ranges)
    full = lambda shape: pl.BlockSpec(shape, lambda n: (0,) * len(shape))
    params = dict(
        scratch_shapes=[
            pltpu.VMEM((angles, depth, columns + 128), jnp.float32),
            pltpu.VMEM((32 * depth, angles * band), jnp.bfloat16),
            pltpu.VMEM((wide_y, angles * band), jnp.bfloat16),
            pltpu.SemaphoreType.DMA((angles,)),
        ],
        grid=(1,),
        compiler_params=pltpu.CompilerParams(vmem_limit_bytes=VMEM_LIMIT),
        cost_estimate=cost(2.0 + depth / 8),
    )
    specs = [SMEM, SMEM, full(proj.shape), ANY, ANY]
    f32 = lambda *shape: jax.ShapeDtypeStruct(shape, jnp.float32)
    if recv is None:
        shape = (4, 4, 2, depth, wide_y)
        return pl.pallas_call(
            functools.partial(other_kernel, ranges),
            out_shape=f32(*shape),
            in_specs=specs,
            out_specs=full(shape),
            **params,
        )(pos, offsets, proj, weights, token)
    shapes = [(n, 2, depth, wide_y) for n in (4, 4, 2, 2, 4)]
    return pl.pallas_call(
        functools.partial(mine_kernel, ranges),
        out_shape=[f32(*s) for s in shapes],
        in_specs=specs + [full(recv.shape)],
        out_specs=[full(s) for s in shapes],
        **params,
    )(pos, offsets, proj, weights, token, recv)


def conduct_kernel(table, phase, contact, token, out):
    for r in range(phase.shape[0]):
        for z in range(0, phase.shape[1], 8):
            label = phase[r, z:z + 8, :]
            other = contact[r, z:z + 8, :]
            odd, upper = (other & 1) == 1, other >= 2
            odd_row, upper_row = (label & 1) == 1, label >= 2
            rows = [
                jnp.where(
                    upper,
                    jnp.where(odd, table[p, 3], table[p, 2]),
                    jnp.where(odd, table[p, 1], table[p, 0]),
                )
                for p in range(4)
            ]
            out[r, z:z + 8, :] = jnp.where(
                upper_row,
                jnp.where(odd_row, rows[3], rows[2]),
                jnp.where(odd_row, rows[1], rows[0]),
            )


def conductivities(table, phase, contact, token):
    return pl.pallas_call(
        conduct_kernel,
        out_shape=jax.ShapeDtypeStruct(phase.shape, jnp.float32),
        in_specs=[SMEM, VMEM, VMEM, ANY],
        out_specs=VMEM,
        cost_estimate=cost(2.0),
    )(table, phase, contact, token)


def swap_kernel(core, left, value, right, token, given):
    @pl.when(core[0] == 0)
    def _():
        given[:2] = value[...]
        given[2:] = right[...]

    @pl.when(core[0] != 0)
    def _():
        given[:2] = left[...]
        given[2:] = value[...]


def widened(core, value, token, us=1.0):
    left = shift_line(value, "ang", 2)
    right = shift_line(value, "ang", -2)
    _, depth, columns = value.shape
    given = pl.pallas_call(
        swap_kernel,
        out_shape=jax.ShapeDtypeStruct((4, depth, columns), jnp.float32),
        in_specs=[SMEM] + [VMEM] * 3 + [ANY],
        out_specs=VMEM,
        compiler_params=pltpu.CompilerParams(vmem_limit_bytes=VMEM_LIMIT),
        cost_estimate=cost(us),
    )(core.reshape(1), left, value, right, token)
    got = shift_ang(given, dc=1)
    return [left, got, value, right], given


def ends_kernel(*refs):
    top, bottom = refs[8:]
    for n in range(2):
        left, got, value, right = refs[4 * n:4 * n + 4]
        depth = value.shape[1]
        for out, z in ((top, slice(depth - 4, depth)), (bottom, slice(0, 4))):
            out[n, 0:2] = left[:, z]
            out[n, 2:4] = got[:2, z]
            out[n, 4:6] = value[:, z]
            out[n, 6:8] = got[2:, z]
            out[n, 8:10] = right[:, z]


def ends(cond, outer):
    shape = (2, 10, 4, outer[0].shape[2])
    top, bottom = small(ends_kernel, [shape] * 2, [*cond, *outer], us=3.0)
    return shift_line(top, "gz", 1), shift_line(bottom, "gz", -1)


def fill(scratch, groups, low, high, kind):
    rows, tall, columns = scratch.shape
    zeros = jnp.zeros((rows, 8, columns), jnp.float32)
    scratch[:, :8] = zeros
    scratch[:, tall - 8:] = zeros
    scratch[:, 4:8] = low[kind]
    scratch[:, tall - 8:tall - 4] = high[kind]
    for ranges, (left, got, value, right) in groups:
        at = 0
        for first, count in ranges:
            z, own = slice(8 + first, 8 + first + count), slice(at, at + count)
            scratch[0:2, z] = left[:, own]
            scratch[2:4, z] = got[:2, own]
            scratch[4:6, z] = value[:, own]
            scratch[6:8, z] = got[2:, own]
            scratch[8:10, z] = right[:, own]
            at += count


def face_of(a, b):
    total = a + b
    positive = total > 0.0
    return jnp.where(positive, 2.0 * a * b / jnp.where(positive, total, 1.0), 0.0)


def next_z(sub, here, above):
    return jnp.where(sub == 7, pltpu.roll(above, 7, 0), pltpu.roll(here, 7, 0))


def faces_kernel(left, got, value, right, low, high, token, fx, fy, fz, con):
    fill(con, [(((0, value.shape[1]),), (left, got, value, right))], low, high, 0)
    rows, tall, columns = con.shape
    tiles = tall // 8
    lane = lax.broadcasted_iota(jnp.int32, (8, columns), 1)
    sub = lax.broadcasted_iota(jnp.int32, (8, columns), 0)

    def face_body(r, carry):
        here = con[r, 0:8, :]
        for t in range(tiles):
            z = slice(8 * t, 8 * t + 8)
            above = con[r, 8 * t + 8:8 * t + 16, :] if t + 1 < tiles else jnp.zeros_like(here)
            along_y = pltpu.roll(here, columns - 1, 1)
            fy[r, z, :] = jnp.where(lane == columns - 1, 0.0, face_of(here, along_y))
            fz[r, z, :] = face_of(here, next_z(sub, here, above))
            fx[r, z, :] = face_of(here, con[jnp.minimum(r + 1, rows - 1), z, :])
            here = above
        return carry

    lax.fori_loop(0, rows, face_body, 0)


def faces(cond, low, high, token):
    _, depth, columns = cond[2].shape
    shape = (2 * STEPS + 2, depth + 16, columns)
    return pl.pallas_call(
        faces_kernel,
        out_shape=[jax.ShapeDtypeStruct(shape, jnp.float32)] * 3,
        in_specs=[VMEM] * 6 + [ANY],
        out_specs=[VMEM] * 3,
        scratch_shapes=[pltpu.VMEM(shape, jnp.float32)],
        compiler_params=pltpu.CompilerParams(vmem_limit_bytes=VMEM_LIMIT),
        cost_estimate=cost(6.0),
    )(*cond, low, high, token)


def heat_kernel(chunks, *refs):
    count = 4 * len(chunks)
    parts, (low, high, fx, fy, fz, volume, out, field, other) = refs[:count], refs[count:]
    groups = [(c, parts[4 * n:4 * n + 4]) for n, c in enumerate(chunks)]
    fill(field, groups, low, high, 1)
    volume[...] = field[STEPS:STEPS + volume.shape[0], 8:8 + volume.shape[1], :]
    rows, tall, columns = field.shape
    tiles = tall // 8
    sub = lax.broadcasted_iota(jnp.int32, (8, columns), 0)
    source, target = field, other
    for step in range(1, STEPS + 1):
        last = step == STEPS
        first_tile, end_tile = (1, tiles - 1) if last else (0, tiles)

        def row_body(r, carry, source=source, target=target, last=last, first_tile=first_tile, end_tile=end_tile):
            if first_tile:
                before = source[r, 8 * first_tile - 8:8 * first_tile, :]
                here = source[r, 8 * first_tile:8 * first_tile + 8, :]
                flux_before = fz[r, 8 * first_tile - 8:8 * first_tile, :] * (
                    next_z(sub, before, here) - before
                )
            else:
                here = source[r, 0:8, :]
                flux_before = jnp.zeros_like(here)
            for t in range(first_tile, end_tile):
                z = slice(8 * t, 8 * t + 8)
                above = source[r, 8 * t + 8:8 * t + 16, :] if t + 1 < tiles else jnp.zeros_like(here)
                flux_x = fx[r, z, :] * (source[r + 1, z, :] - here)
                flux_x -= fx[r - 1, z, :] * (here - source[r - 1, z, :])
                flux_y = fy[r, z, :] * (pltpu.roll(here, columns - 1, 1) - here)
                flux_y -= pltpu.roll(flux_y, 1, 1)
                flux = fz[r, z, :] * (next_z(sub, here, above) - here)
                flux_z = flux - jnp.where(sub == 0, pltpu.roll(flux_before, 1, 0), pltpu.roll(flux, 1, 0))
                value = here + STEP_SIZE * (flux_x + flux_y + flux_z)
                if last:
                    out[r - STEPS, 8 * t - 8:8 * t, :] = value
                else:
                    target[r, z, :] = value
                here, flux_before = above, flux
            return carry

        lax.fori_loop(step, rows - step, row_body, 0)
        source, target = target, source


def conduct_heat(groups, low, high, face_arrays):
    rows, tall, columns = face_arrays[0].shape
    parts = [p for _, group in groups for p in group]
    return pl.pallas_call(
        functools.partial(heat_kernel, [c for c, _ in groups]),
        out_shape=[jax.ShapeDtypeStruct((rows - 2 * STEPS, tall - 16, columns), jnp.float32)] * 2,
        in_specs=[VMEM] * (len(parts) + 5),
        out_specs=[VMEM] * 2,
        scratch_shapes=[pltpu.VMEM((rows, tall, columns), jnp.float32)] * 2,
        compiler_params=pltpu.CompilerParams(vmem_limit_bytes=VMEM_LIMIT),
        cost_estimate=cost(9.0),
    )(*parts, low, high, *face_arrays)


def second_kernel(holdp, fromp, holdm, fromm, token, outp, outm):
    outp[...] = holdp[...] + fromp[:2]
    outm[...] = holdm[...] + fromm[:2]


def ring_kernel(home, lastp, fromp, lastm, fromm, token, near, far):
    near[0] = home[0] + lastp[0] + fromm[2]
    far[0] = home[1] + lastp[1] + fromm[3]
    near[1] = home[2] + lastm[0] + fromp[2]
    far[1] = home[3] + lastm[1] + fromp[3]


def middle_kernel(near, got, token, out):
    out[...] = near[1] + got[1]


def volume_kernel(near, got, last, token, out):
    out[...] = near[0] + got[0] + last[...]


def small(body, outs, inputs, tokens=(), us=1.0):
    return pl.pallas_call(
        body,
        out_shape=[jax.ShapeDtypeStruct(o, jnp.float32) for o in outs],
        in_specs=[VMEM] * len(inputs) + [ANY] * len(tokens),
        out_specs=[VMEM] * len(outs),
        compiler_params=pltpu.CompilerParams(vmem_limit_bytes=VMEM_LIMIT),
        cost_estimate=cost(us),
    )(*inputs, *tokens)


class Chunk:
    def __init__(self, args, ranges, token):
        self.args, self.ranges = args, ranges
        self.recv = shift_ang(backproject(*args, ranges, token), dc=1)

    def first(self, token):
        *send, holdp, holdm, self.home = backproject(
            *self.args, self.ranges, token, self.recv
        )
        self.hold = holdp, holdm
        self.fromp = shift_ang(send[0], dx=1)
        self.fromm = shift_ang(send[1], dx=-1)
        return self.home

    def second(self, token):
        holdp, holdm = self.hold
        outs = small(
            second_kernel, [holdp.shape] * 2, [holdp, self.fromp, holdm, self.fromm], [token]
        )
        self.lastp = shift_ang(outs[0], dx=1)
        self.lastm = shift_ang(outs[1], dx=-1)
        return outs[0]

    def near_z(self, token, us=1.5):
        inputs = [self.home, self.lastp, self.fromp, self.lastm, self.fromm]
        shape = (2, *self.home.shape[1:])
        self.near, far = small(ring_kernel, [shape] * 2, inputs, [token], us=us)
        self.got = shift_ang(far, dz=1)
        return self.near

    def far_z(self, token):
        (out,) = small(middle_kernel, [self.home.shape[1:]], [self.near, self.got], [token])
        self.last = shift_ang(out, dz=2)
        return out

    def volume(self, token, us=1.0):
        parts = [self.near, self.got, self.last]
        return small(volume_kernel, [self.home.shape[1:]], parts, [token], us=us)[0]


def local(projections, band_weights, band_offsets, phase, contact, conductivity_table):
    ang = lax.axis_index("ang")
    core = ang & 1
    pos = jnp.stack([ang >> 3, (ang >> 1) & 3, core]).astype(jnp.int32)
    args = (pos, band_offsets, projections, band_weights)
    conduct = conductivities(conductivity_table, phase, contact, pos)
    outer = Chunk(args, CHUNKS[0], conduct)
    cond, token = widened(core, conduct, pos, us=SWAP_US)
    outer.first(pos)
    middle = Chunk(args, CHUNKS[1], pos)
    middle.first(outer.second(token))
    outer.near_z(pos, us=NEAR_US)
    token = outer.far_z(middle.second(pos))
    token = middle.near_z(token)
    outer_volume = outer.volume(token)
    token = middle.far_z(outer_volume)
    outer_rows, _ = widened(core, outer_volume, token)
    low, high = ends(cond, outer_rows)
    middle_volume = middle.volume(outer_volume, us=4.0)
    face_arrays = faces(cond, low, high, middle_volume)
    middle_rows, _ = widened(core, middle_volume, face_arrays[0])
    return conduct_heat(list(zip(CHUNKS, (outer_rows, middle_rows))), low, high, face_arrays)


def solution(mesh):
    in_specs = (
        P("ang", "gz", None),
        P("ang", None, None),
        P("ang", None),
        P("ang", "gz", None),
        P("ang", "gz", None),
        P(),
    )
    out_specs = (P("ang", "gz", None), P("ang", "gz", None))
    return jax.shard_map(local, mesh=mesh, in_specs=in_specs, out_specs=out_specs, check_vma=False)
```

```python
import functools
import jax
import jax.numpy as jnp
from jax import lax
from jax.experimental import pallas as pl
from jax.experimental.pallas import tpu as pltpu
from jax.sharding import PartitionSpec as P

STEPS = 4
STEP_SIZE = 0.15
CHUNKS = (((0, 16), (48, 16)), ((16, 32),))
TILE = 256
NEAR_US = 9.0
TOKEN = (8, 128)
SWAP_US = 40.0
ZL, X, C = 4, 4, 2
VMEM_LIMIT = 26 * 1024 * 1024


def shift_ang(value, dz=0, dx=0, dc=0):
    perm = []
    for z in range(ZL):
        for x in range(X):
            for c in range(C):
                src = (z * X + x) * C + c
                dst = ((z ^ dz) * X + (x + dx) % X) * C + (c ^ dc)
                perm.append((src, dst))
    return lax.ppermute(value, "ang", perm)


def shift_line(value, axis, step):
    count = lax.axis_size(axis)
    perm = [(i, i + step) for i in range(count) if 0 <= i + step < count]
    return lax.ppermute(value, axis, perm)


def gather(ranges, pos, offsets, proj, weights, wide, bands, flat, sems, core):
    angles, _, columns = proj.shape
    depth = wide.shape[1]
    copies = [
        pltpu.make_async_copy(weights.at[a], flat.at[:, a * 128:(a + 1) * 128], sems.at[a])
        for a in range(angles)
    ]
    for copy in copies:
        copy.start()
    wide[:, :, columns:] = jnp.zeros((angles, depth, 128), jnp.float32)
    for a in range(angles):
        at = 0
        for first, count in ranges:
            wide[a, at:at + count, :columns] = proj[a, first:first + count, :].astype(jnp.float32)
            at += count
    lane = lax.broadcasted_iota(jnp.int32, (depth, 128), 1)

    def row_body(row, carry):
        dx, dz, i = row >> 3, (row >> 1) & 3, row & 1
        owner = (
            (pos[0] ^ dz) * (X * C * 2)
            + ((pos[1] + dx) & (X - 1)) * (C * 2)
            + core * 2
            + i
        )
        for a in range(angles):
            off = offsets[a, owner]
            base = pl.multiple_of((off >> 7) << 7, 128)
            rem = off & 127
            low = wide[a, :, pl.ds(base, 128)]
            high = wide[a, :, pl.ds(pl.multiple_of(base + 128, 128), 128)]
            band = pltpu.roll(jnp.where(lane < rem, high, low), (128 - rem) & 127, 1)
            bands[pl.ds(pl.multiple_of(row * depth, depth), depth), a * 128:(a + 1) * 128] = (
                band.astype(jnp.bfloat16)
            )
        return carry

    lax.fori_loop(0, bands.shape[0] // depth, row_body, 0, unroll=4)
    for copy in copies:
        copy.wait()


def product(bands, flat, store):
    for n in range(0, flat.shape[0], TILE):
        out = lax.dot_general(
            bands[...],
            flat[n:n + TILE, :],
            (((1,), (1,)), ((), ())),
            preferred_element_type=jnp.float32,
        )
        store(out.reshape(4, 4, 2, bands.shape[0] // 32, TILE), slice(n, n + TILE))


def other_kernel(ranges, pos, offsets, proj, weights, token, out, done, wide, bands, flat, sems):
    done[...] = jnp.zeros(done.shape, jnp.float32)

    def store(value, cols):
        out[:, :, :, :, cols] = value

    gather(ranges, pos, offsets, proj, weights, wide, bands, flat, sems, 1 - pos[2])
    product(bands, flat, store)


def mine_kernel(
    ranges,
    pos,
    offsets,
    proj,
    weights,
    token,
    recv,
    sendp,
    sendm,
    holdp,
    holdm,
    home,
    wide,
    bands,
    flat,
    sems,
):
    def store(value, cols):
        value = value + recv[:, :, :, :, cols]
        sendp[:2, :, :, cols] = value[2, :2]
        sendp[2:, :, :, cols] = value[1, 2:]
        sendm[:2, :, :, cols] = value[2, 2:]
        sendm[2:, :, :, cols] = value[3, :2]
        holdp[:, :, :, cols] = value[1, :2]
        holdm[:, :, :, cols] = value[3, 2:]
        home[:, :, :, cols] = value[0]

    gather(ranges, pos, offsets, proj, weights, wide, bands, flat, sems, pos[2])
    product(bands, flat, store)


SMEM = pl.BlockSpec(memory_space=pltpu.SMEM)
VMEM = pl.BlockSpec(memory_space=pltpu.VMEM)
ANY = pl.BlockSpec(memory_space=pl.ANY)


def cost(us):
    return pl.CostEstimate(flops=int(us * 1.1e9), bytes_accessed=2**20, transcendentals=0)


def backproject(pos, offsets, proj, weights, ranges, token, recv=None, us=6.0):
    angles, _, columns = proj.shape
    wide_y, band = weights.shape[1:]
    depth = sum(count for _, count in ranges)
    full = lambda shape: pl.BlockSpec(shape, lambda n: (0,) * len(shape))
    params = dict(
        scratch_shapes=[
            pltpu.VMEM((angles, depth, columns + 128), jnp.float32),
            pltpu.VMEM((32 * depth, angles * band), jnp.bfloat16),
            pltpu.VMEM((wide_y, angles * band), jnp.bfloat16),
            pltpu.SemaphoreType.DMA((angles,)),
        ],
        grid=(1,),
        compiler_params=pltpu.CompilerParams(vmem_limit_bytes=VMEM_LIMIT),
        cost_estimate=cost(us),
    )
    specs = [SMEM, SMEM, full(proj.shape), ANY, ANY]
    f32 = lambda *shape: jax.ShapeDtypeStruct(shape, jnp.float32)
    if recv is None:
        shape = (4, 4, 2, depth, wide_y)
        return pl.pallas_call(
            functools.partial(other_kernel, ranges),
            out_shape=[f32(*shape), f32(*TOKEN)],
            in_specs=specs,
            out_specs=[full(shape), full(TOKEN)],
            **params,
        )(pos, offsets, proj, weights, token)
    shapes = [(n, 2, depth, wide_y) for n in (4, 4, 2, 2, 4)]
    return pl.pallas_call(
        functools.partial(mine_kernel, ranges),
        out_shape=[f32(*s) for s in shapes],
        in_specs=specs + [full(recv.shape)],
        out_specs=[full(s) for s in shapes],
        **params,
    )(pos, offsets, proj, weights, token, recv)


def conduct_kernel(table, phase, contact, token, out):
    for r in range(phase.shape[0]):
        for z in range(0, phase.shape[1], 8):
            label = phase[r, z:z + 8, :]
            other = contact[r, z:z + 8, :]
            odd, upper = (other & 1) == 1, other >= 2
            odd_row, upper_row = (label & 1) == 1, label >= 2
            rows = [
                jnp.where(
                    upper,
                    jnp.where(odd, table[p, 3], table[p, 2]),
                    jnp.where(odd, table[p, 1], table[p, 0]),
                )
                for p in range(4)
            ]
            out[r, z:z + 8, :] = jnp.where(
                upper_row,
                jnp.where(odd_row, rows[3], rows[2]),
                jnp.where(odd_row, rows[1], rows[0]),
            )


def conductivities(table, phase, contact, token):
    return pl.pallas_call(
        conduct_kernel,
        out_shape=jax.ShapeDtypeStruct(phase.shape, jnp.float32),
        in_specs=[SMEM, VMEM, VMEM, ANY],
        out_specs=VMEM,
        cost_estimate=cost(2.0),
    )(table, phase, contact, token)


def swap_kernel(core, left, value, right, token, given):
    @pl.when(core[0] == 0)
    def _():
        given[:2] = value[...]
        given[2:] = right[...]

    @pl.when(core[0] != 0)
    def _():
        given[:2] = left[...]
        given[2:] = value[...]


def widened(core, value, token, us=1.0):
    left = shift_line(value, "ang", 2)
    right = shift_line(value, "ang", -2)
    _, depth, columns = value.shape
    given = pl.pallas_call(
        swap_kernel,
        out_shape=jax.ShapeDtypeStruct((4, depth, columns), jnp.float32),
        in_specs=[SMEM] + [VMEM] * 3 + [ANY],
        out_specs=VMEM,
        compiler_params=pltpu.CompilerParams(vmem_limit_bytes=VMEM_LIMIT),
        cost_estimate=cost(us),
    )(core.reshape(1), left, value, right, token)
    got = shift_ang(given, dc=1)
    return [left, got, value, right], given


def ends_kernel(*refs):
    top, bottom = refs[8:]
    for n in range(2):
        left, got, value, right = refs[4 * n:4 * n + 4]
        depth = value.shape[1]
        for out, z in ((top, slice(depth - 4, depth)), (bottom, slice(0, 4))):
            out[n, 0:2] = left[:, z]
            out[n, 2:4] = got[:2, z]
            out[n, 4:6] = value[:, z]
            out[n, 6:8] = got[2:, z]
            out[n, 8:10] = right[:, z]


def ends(cond, outer):
    shape = (2, 10, 4, outer[0].shape[2])
    top, bottom = small(ends_kernel, [shape] * 2, [*cond, *outer], us=3.0)
    return shift_line(top, "gz", 1), shift_line(bottom, "gz", -1)


def fill(scratch, groups, low, high, kind):
    rows, tall, columns = scratch.shape
    zeros = jnp.zeros((rows, 8, columns), jnp.float32)
    scratch[:, :8] = zeros
    scratch[:, tall - 8:] = zeros
    scratch[:, 4:8] = low[kind]
    scratch[:, tall - 8:tall - 4] = high[kind]
    for ranges, (left, got, value, right) in groups:
        at = 0
        for first, count in ranges:
            z, own = slice(8 + first, 8 + first + count), slice(at, at + count)
            scratch[0:2, z] = left[:, own]
            scratch[2:4, z] = got[:2, own]
            scratch[4:6, z] = value[:, own]
            scratch[6:8, z] = got[2:, own]
            scratch[8:10, z] = right[:, own]
            at += count


def face_of(a, b):
    total = a + b
    positive = total > 0.0
    return jnp.where(positive, 2.0 * a * b / jnp.where(positive, total, 1.0), 0.0)


def next_z(sub, here, above):
    return jnp.where(sub == 7, pltpu.roll(above, 7, 0), pltpu.roll(here, 7, 0))


def faces_kernel(left, got, value, right, low, high, token, fx, fy, fz, con):
    fill(con, [(((0, value.shape[1]),), (left, got, value, right))], low, high, 0)
    rows, tall, columns = con.shape
    tiles = tall // 8
    lane = lax.broadcasted_iota(jnp.int32, (8, columns), 1)
    sub = lax.broadcasted_iota(jnp.int32, (8, columns), 0)

    def face_body(r, carry):
        here = con[r, 0:8, :]
        for t in range(tiles):
            z = slice(8 * t, 8 * t + 8)
            above = con[r, 8 * t + 8:8 * t + 16, :] if t + 1 < tiles else jnp.zeros_like(here)
            along_y = pltpu.roll(here, columns - 1, 1)
            fy[r, z, :] = jnp.where(lane == columns - 1, 0.0, face_of(here, along_y))
            fz[r, z, :] = face_of(here, next_z(sub, here, above))
            fx[r, z, :] = face_of(here, con[jnp.minimum(r + 1, rows - 1), z, :])
            here = above
        return carry

    lax.fori_loop(0, rows, face_body, 0)


def faces(cond, low, high, token):
    _, depth, columns = cond[2].shape
    shape = (2 * STEPS + 2, depth + 16, columns)
    return pl.pallas_call(
        faces_kernel,
        out_shape=[jax.ShapeDtypeStruct(shape, jnp.float32)] * 3,
        in_specs=[VMEM] * 6 + [ANY],
        out_specs=[VMEM] * 3,
        scratch_shapes=[pltpu.VMEM(shape, jnp.float32)],
        compiler_params=pltpu.CompilerParams(vmem_limit_bytes=VMEM_LIMIT),
        cost_estimate=cost(6.0),
    )(*cond, low, high, token)


def heat_kernel(chunks, *refs):
    count = 4 * len(chunks)
    parts, (low, high, fx, fy, fz, volume, out, field, other) = refs[:count], refs[count:]
    groups = [(c, parts[4 * n:4 * n + 4]) for n, c in enumerate(chunks)]
    fill(field, groups, low, high, 1)
    volume[...] = field[STEPS:STEPS + volume.shape[0], 8:8 + volume.shape[1], :]
    rows, tall, columns = field.shape
    tiles = tall // 8
    sub = lax.broadcasted_iota(jnp.int32, (8, columns), 0)
    source, target = field, other
    for step in range(1, STEPS + 1):
        last = step == STEPS
        first_tile, end_tile = (1, tiles - 1) if last else (0, tiles)

        def row_body(r, carry, source=source, target=target, last=last, first_tile=first_tile, end_tile=end_tile):
            if first_tile:
                before = source[r, 8 * first_tile - 8:8 * first_tile, :]
                here = source[r, 8 * first_tile:8 * first_tile + 8, :]
                flux_before = fz[r, 8 * first_tile - 8:8 * first_tile, :] * (
                    next_z(sub, before, here) - before
                )
            else:
                here = source[r, 0:8, :]
                flux_before = jnp.zeros_like(here)
            for t in range(first_tile, end_tile):
                z = slice(8 * t, 8 * t + 8)
                above = source[r, 8 * t + 8:8 * t + 16, :] if t + 1 < tiles else jnp.zeros_like(here)
                flux_x = fx[r, z, :] * (source[r + 1, z, :] - here)
                flux_x -= fx[r - 1, z, :] * (here - source[r - 1, z, :])
                flux_y = fy[r, z, :] * (pltpu.roll(here, columns - 1, 1) - here)
                flux_y -= pltpu.roll(flux_y, 1, 1)
                flux = fz[r, z, :] * (next_z(sub, here, above) - here)
                flux_z = flux - jnp.where(sub == 0, pltpu.roll(flux_before, 1, 0), pltpu.roll(flux, 1, 0))
                value = here + STEP_SIZE * (flux_x + flux_y + flux_z)
                if last:
                    out[r - STEPS, 8 * t - 8:8 * t, :] = value
                else:
                    target[r, z, :] = value
                here, flux_before = above, flux
            return carry

        lax.fori_loop(step, rows - step, row_body, 0)
        source, target = target, source


def conduct_heat(groups, low, high, face_arrays):
    rows, tall, columns = face_arrays[0].shape
    parts = [p for _, group in groups for p in group]
    return pl.pallas_call(
        functools.partial(heat_kernel, [c for c, _ in groups]),
        out_shape=[jax.ShapeDtypeStruct((rows - 2 * STEPS, tall - 16, columns), jnp.float32)] * 2,
        in_specs=[VMEM] * (len(parts) + 5),
        out_specs=[VMEM] * 2,
        scratch_shapes=[pltpu.VMEM((rows, tall, columns), jnp.float32)] * 2,
        compiler_params=pltpu.CompilerParams(vmem_limit_bytes=VMEM_LIMIT),
        cost_estimate=cost(9.0),
    )(*parts, low, high, *face_arrays)


def second_kernel(holdp, fromp, holdm, fromm, token, outp, outm):
    outp[...] = holdp[...] + fromp[:2]
    outm[...] = holdm[...] + fromm[:2]


def ring_kernel(home, lastp, fromp, lastm, fromm, token, near, far):
    near[0] = home[0] + lastp[0] + fromm[2]
    far[0] = home[1] + lastp[1] + fromm[3]
    near[1] = home[2] + lastm[0] + fromp[2]
    far[1] = home[3] + lastm[1] + fromp[3]


def middle_kernel(near, got, token, out):
    out[...] = near[1] + got[1]


def volume_kernel(near, got, last, token, out):
    out[...] = near[0] + got[0] + last[...]


def small(body, outs, inputs, tokens=(), us=1.0):
    return pl.pallas_call(
        body,
        out_shape=[jax.ShapeDtypeStruct(o, jnp.float32) for o in outs],
        in_specs=[VMEM] * len(inputs) + [ANY] * len(tokens),
        out_specs=[VMEM] * len(outs),
        compiler_params=pltpu.CompilerParams(vmem_limit_bytes=VMEM_LIMIT),
        cost_estimate=cost(us),
    )(*inputs, *tokens)


class Chunk:
    def __init__(self, args, ranges, token):
        self.args, self.ranges = args, ranges
        theirs, self.started = backproject(*args, ranges, token)
        self.recv = shift_ang(theirs, dc=1)

    def first(self, token, us=6.0):
        *send, holdp, holdm, self.home = backproject(
            *self.args, self.ranges, token, self.recv, us=us
        )
        self.hold = holdp, holdm
        self.fromp = shift_ang(send[0], dx=1)
        self.fromm = shift_ang(send[1], dx=-1)
        return self.home

    def second(self, token):
        holdp, holdm = self.hold
        outs = small(
            second_kernel, [holdp.shape] * 2, [holdp, self.fromp, holdm, self.fromm], [token]
        )
        self.lastp = shift_ang(outs[0], dx=1)
        self.lastm = shift_ang(outs[1], dx=-1)
        return outs[0]

    def near_z(self, token, us=1.5):
        inputs = [self.home, self.lastp, self.fromp, self.lastm, self.fromm]
        shape = (2, *self.home.shape[1:])
        self.near, far = small(ring_kernel, [shape] * 2, inputs, [token], us=us)
        self.got = shift_ang(far, dz=1)
        return self.near

    def far_z(self, token):
        (out,) = small(middle_kernel, [self.home.shape[1:]], [self.near, self.got], [token])
        self.last = shift_ang(out, dz=2)
        return out

    def volume(self, token, us=1.0):
        parts = [self.near, self.got, self.last]
        return small(volume_kernel, [self.home.shape[1:]], parts, [token], us=us)[0]


def local(projections, band_weights, band_offsets, phase, contact, conductivity_table):
    ang = lax.axis_index("ang")
    core = ang & 1
    pos = jnp.stack([ang >> 3, (ang >> 1) & 3, core]).astype(jnp.int32)
    args = (pos, band_offsets, projections, band_weights)
    conduct = conductivities(conductivity_table, phase, contact, pos)
    outer = Chunk(args, CHUNKS[0], conduct)
    cond, token = widened(core, conduct, pos, us=SWAP_US)
    middle = Chunk(args, CHUNKS[1], pos)
    outer.first(middle.started, us=1.0)
    middle.first(outer.second(token))
    outer.near_z(pos, us=NEAR_US)
    token = outer.far_z(middle.second(pos))
    token = middle.near_z(token)
    outer_volume = outer.volume(token)
    token = middle.far_z(outer_volume)
    outer_rows, _ = widened(core, outer_volume, token)
    low, high = ends(cond, outer_rows)
    middle_volume = middle.volume(outer_volume, us=4.0)
    face_arrays = faces(cond, low, high, middle_volume)
    middle_rows, _ = widened(core, middle_volume, face_arrays[0])
    return conduct_heat(list(zip(CHUNKS, (outer_rows, middle_rows))), low, high, face_arrays)


def solution(mesh):
    in_specs = (
        P("ang", "gz", None),
        P("ang", None, None),
        P("ang", None),
        P("ang", "gz", None),
        P("ang", "gz", None),
        P(),
    )
    out_specs = (P("ang", "gz", None), P("ang", "gz", None))
    return jax.shard_map(local, mesh=mesh, in_specs=in_specs, out_specs=out_specs, check_vma=False)
```

```python
import functools
import jax
import jax.numpy as jnp
from jax import lax
from jax.experimental import pallas as pl
from jax.experimental.pallas import tpu as pltpu
from jax.sharding import PartitionSpec as P

STEPS = 4
STEP_SIZE = 0.15
CHUNKS = (((0, 16), (48, 16)), ((16, 32),))
TILE = 256
NEAR_US = 9.0
TOKEN = (8, 128)
SWAP_US = 40.0
ZL, X, C = 4, 4, 2
VMEM_LIMIT = 26 * 1024 * 1024


def shift_ang(value, dz=0, dx=0, dc=0):
    perm = []
    for z in range(ZL):
        for x in range(X):
            for c in range(C):
                src = (z * X + x) * C + c
                dst = ((z ^ dz) * X + (x + dx) % X) * C + (c ^ dc)
                perm.append((src, dst))
    return lax.ppermute(value, "ang", perm)


def shift_line(value, axis, step):
    count = lax.axis_size(axis)
    perm = [(i, i + step) for i in range(count) if 0 <= i + step < count]
    return lax.ppermute(value, axis, perm)


def gather(ranges, pos, offsets, proj, weights, wide, bands, flat, sems, core):
    angles, _, columns = proj.shape
    depth = wide.shape[1]
    copies = [
        pltpu.make_async_copy(weights.at[a], flat.at[:, a * 128:(a + 1) * 128], sems.at[a])
        for a in range(angles)
    ]
    for copy in copies:
        copy.start()
    wide[:, :, columns:] = jnp.zeros((angles, depth, 128), jnp.float32)
    for a in range(angles):
        at = 0
        for first, count in ranges:
            wide[a, at:at + count, :columns] = proj[a, first:first + count, :].astype(jnp.float32)
            at += count
    lane = lax.broadcasted_iota(jnp.int32, (depth, 128), 1)

    def row_body(row, carry):
        dx, dz, i = row >> 3, (row >> 1) & 3, row & 1
        owner = (
            (pos[0] ^ dz) * (X * C * 2)
            + ((pos[1] + dx) & (X - 1)) * (C * 2)
            + core * 2
            + i
        )
        for a in range(angles):
            off = offsets[a, owner]
            base = pl.multiple_of((off >> 7) << 7, 128)
            rem = off & 127
            low = wide[a, :, pl.ds(base, 128)]
            high = wide[a, :, pl.ds(pl.multiple_of(base + 128, 128), 128)]
            band = pltpu.roll(jnp.where(lane < rem, high, low), (128 - rem) & 127, 1)
            bands[pl.ds(pl.multiple_of(row * depth, depth), depth), a * 128:(a + 1) * 128] = (
                band.astype(jnp.bfloat16)
            )
        return carry

    lax.fori_loop(0, bands.shape[0] // depth, row_body, 0, unroll=4)
    for copy in copies:
        copy.wait()


def product(bands, flat, store):
    for n in range(0, flat.shape[0], TILE):
        out = lax.dot_general(
            bands[...],
            flat[n:n + TILE, :],
            (((1,), (1,)), ((), ())),
            preferred_element_type=jnp.float32,
        )
        store(out.reshape(4, 4, 2, bands.shape[0] // 32, TILE), slice(n, n + TILE))


def other_kernel(ranges, pos, offsets, proj, weights, token, out, done, wide, bands, flat, sems):
    done[...] = jnp.zeros(done.shape, jnp.float32)

    def store(value, cols):
        out[:, :, :, :, cols] = value

    gather(ranges, pos, offsets, proj, weights, wide, bands, flat, sems, 1 - pos[2])
    product(bands, flat, store)


def mine_kernel(
    ranges,
    pos,
    offsets,
    proj,
    weights,
    token,
    recv,
    sendp,
    sendm,
    holdp,
    holdm,
    home,
    wide,
    bands,
    flat,
    sems,
):
    def store(value, cols):
        value = value + recv[:, :, :, :, cols]
        sendp[:2, :, :, cols] = value[2, :2]
        sendp[2:, :, :, cols] = value[1, 2:]
        sendm[:2, :, :, cols] = value[2, 2:]
        sendm[2:, :, :, cols] = value[3, :2]
        holdp[:, :, :, cols] = value[1, :2]
        holdm[:, :, :, cols] = value[3, 2:]
        home[:, :, :, cols] = value[0]

    gather(ranges, pos, offsets, proj, weights, wide, bands, flat, sems, pos[2])
    product(bands, flat, store)


SMEM = pl.BlockSpec(memory_space=pltpu.SMEM)
VMEM = pl.BlockSpec(memory_space=pltpu.VMEM)
ANY = pl.BlockSpec(memory_space=pl.ANY)


def cost(us):
    return pl.CostEstimate(flops=int(us * 1.1e9), bytes_accessed=2**20, transcendentals=0)


def backproject(pos, offsets, proj, weights, ranges, token, recv=None, us=6.0):
    angles, _, columns = proj.shape
    wide_y, band = weights.shape[1:]
    depth = sum(count for _, count in ranges)
    full = lambda shape: pl.BlockSpec(shape, lambda n: (0,) * len(shape))
    params = dict(
        scratch_shapes=[
            pltpu.VMEM((angles, depth, columns + 128), jnp.float32),
            pltpu.VMEM((32 * depth, angles * band), jnp.bfloat16),
            pltpu.VMEM((wide_y, angles * band), jnp.bfloat16),
            pltpu.SemaphoreType.DMA((angles,)),
        ],
        grid=(1,),
        compiler_params=pltpu.CompilerParams(vmem_limit_bytes=VMEM_LIMIT),
        cost_estimate=cost(us),
    )
    specs = [SMEM, SMEM, full(proj.shape), ANY, ANY]
    f32 = lambda *shape: jax.ShapeDtypeStruct(shape, jnp.float32)
    if recv is None:
        shape = (4, 4, 2, depth, wide_y)
        return pl.pallas_call(
            functools.partial(other_kernel, ranges),
            out_shape=[f32(*shape), f32(*TOKEN)],
            in_specs=specs,
            out_specs=[full(shape), full(TOKEN)],
            **params,
        )(pos, offsets, proj, weights, token)
    shapes = [(n, 2, depth, wide_y) for n in (4, 4, 2, 2, 4)]
    return pl.pallas_call(
        functools.partial(mine_kernel, ranges),
        out_shape=[f32(*s) for s in shapes],
        in_specs=specs + [full(recv.shape)],
        out_specs=[full(s) for s in shapes],
        **params,
    )(pos, offsets, proj, weights, token, recv)


def conduct_kernel(table, phase, contact, token, out, done):
    done[...] = jnp.zeros(done.shape, jnp.float32)
    for r in range(phase.shape[0]):
        for z in range(0, phase.shape[1], 8):
            label = phase[r, z:z + 8, :]
            other = contact[r, z:z + 8, :]
            odd, upper = (other & 1) == 1, other >= 2
            odd_row, upper_row = (label & 1) == 1, label >= 2
            rows = [
                jnp.where(
                    upper,
                    jnp.where(odd, table[p, 3], table[p, 2]),
                    jnp.where(odd, table[p, 1], table[p, 0]),
                )
                for p in range(4)
            ]
            out[r, z:z + 8, :] = jnp.where(
                upper_row,
                jnp.where(odd_row, rows[3], rows[2]),
                jnp.where(odd_row, rows[1], rows[0]),
            )


def conductivities(table, phase, contact, token):
    return pl.pallas_call(
        conduct_kernel,
        out_shape=[jax.ShapeDtypeStruct(v, jnp.float32) for v in (phase.shape, TOKEN)],
        in_specs=[SMEM, VMEM, VMEM, ANY],
        out_specs=[VMEM, VMEM],
        cost_estimate=cost(2.0),
    )(table, phase, contact, token)


def swap_kernel(core, left, value, right, token, given):
    @pl.when(core[0] == 0)
    def _():
        given[:2] = value[...]
        given[2:] = right[...]

    @pl.when(core[0] != 0)
    def _():
        given[:2] = left[...]
        given[2:] = value[...]


def widened(core, value, token, us=1.0):
    left = shift_line(value, "ang", 2)
    right = shift_line(value, "ang", -2)
    _, depth, columns = value.shape
    given = pl.pallas_call(
        swap_kernel,
        out_shape=jax.ShapeDtypeStruct((4, depth, columns), jnp.float32),
        in_specs=[SMEM] + [VMEM] * 3 + [ANY],
        out_specs=VMEM,
        compiler_params=pltpu.CompilerParams(vmem_limit_bytes=VMEM_LIMIT),
        cost_estimate=cost(us),
    )(core.reshape(1), left, value, right, token)
    got = shift_ang(given, dc=1)
    return [left, got, value, right], given


def ends_kernel(*refs):
    top, bottom = refs[8:]
    for n in range(2):
        left, got, value, right = refs[4 * n:4 * n + 4]
        depth = value.shape[1]
        for out, z in ((top, slice(depth - 4, depth)), (bottom, slice(0, 4))):
            out[n, 0:2] = left[:, z]
            out[n, 2:4] = got[:2, z]
            out[n, 4:6] = value[:, z]
            out[n, 6:8] = got[2:, z]
            out[n, 8:10] = right[:, z]


def ends(cond, outer):
    shape = (2, 10, 4, outer[0].shape[2])
    top, bottom = small(ends_kernel, [shape] * 2, [*cond, *outer], us=3.0)
    return shift_line(top, "gz", 1), shift_line(bottom, "gz", -1)


def fill(scratch, groups, low, high, kind):
    rows, tall, columns = scratch.shape
    zeros = jnp.zeros((rows, 8, columns), jnp.float32)
    scratch[:, :8] = zeros
    scratch[:, tall - 8:] = zeros
    scratch[:, 4:8] = low[kind]
    scratch[:, tall - 8:tall - 4] = high[kind]
    for ranges, (left, got, value, right) in groups:
        at = 0
        for first, count in ranges:
            z, own = slice(8 + first, 8 + first + count), slice(at, at + count)
            scratch[0:2, z] = left[:, own]
            scratch[2:4, z] = got[:2, own]
            scratch[4:6, z] = value[:, own]
            scratch[6:8, z] = got[2:, own]
            scratch[8:10, z] = right[:, own]
            at += count


def face_of(a, b):
    total = a + b
    positive = total > 0.0
    return jnp.where(positive, 2.0 * a * b / jnp.where(positive, total, 1.0), 0.0)


def next_z(sub, here, above):
    return jnp.where(sub == 7, pltpu.roll(above, 7, 0), pltpu.roll(here, 7, 0))


def faces_kernel(left, got, value, right, low, high, token, fx, fy, fz, con):
    fill(con, [(((0, value.shape[1]),), (left, got, value, right))], low, high, 0)
    rows, tall, columns = con.shape
    tiles = tall // 8
    lane = lax.broadcasted_iota(jnp.int32, (8, columns), 1)
    sub = lax.broadcasted_iota(jnp.int32, (8, columns), 0)

    def face_body(r, carry):
        here = con[r, 0:8, :]
        for t in range(tiles):
            z = slice(8 * t, 8 * t + 8)
            above = con[r, 8 * t + 8:8 * t + 16, :] if t + 1 < tiles else jnp.zeros_like(here)
            along_y = pltpu.roll(here, columns - 1, 1)
            fy[r, z, :] = jnp.where(lane == columns - 1, 0.0, face_of(here, along_y))
            fz[r, z, :] = face_of(here, next_z(sub, here, above))
            fx[r, z, :] = face_of(here, con[jnp.minimum(r + 1, rows - 1), z, :])
            here = above
        return carry

    lax.fori_loop(0, rows, face_body, 0)


def faces(cond, low, high, token):
    _, depth, columns = cond[2].shape
    shape = (2 * STEPS + 2, depth + 16, columns)
    return pl.pallas_call(
        faces_kernel,
        out_shape=[jax.ShapeDtypeStruct(shape, jnp.float32)] * 3,
        in_specs=[VMEM] * 6 + [ANY],
        out_specs=[VMEM] * 3,
        scratch_shapes=[pltpu.VMEM(shape, jnp.float32)],
        compiler_params=pltpu.CompilerParams(vmem_limit_bytes=VMEM_LIMIT),
        cost_estimate=cost(6.0),
    )(*cond, low, high, token)


def heat_kernel(chunks, *refs):
    count = 4 * len(chunks)
    parts, (low, high, fx, fy, fz, volume, out, field, other) = refs[:count], refs[count:]
    groups = [(c, parts[4 * n:4 * n + 4]) for n, c in enumerate(chunks)]
    fill(field, groups, low, high, 1)
    volume[...] = field[STEPS:STEPS + volume.shape[0], 8:8 + volume.shape[1], :]
    rows, tall, columns = field.shape
    tiles = tall // 8
    sub = lax.broadcasted_iota(jnp.int32, (8, columns), 0)
    source, target = field, other
    for step in range(1, STEPS + 1):
        last = step == STEPS
        first_tile, end_tile = (1, tiles - 1) if last else (0, tiles)

        def row_body(r, carry, source=source, target=target, last=last, first_tile=first_tile, end_tile=end_tile):
            if first_tile:
                before = source[r, 8 * first_tile - 8:8 * first_tile, :]
                here = source[r, 8 * first_tile:8 * first_tile + 8, :]
                flux_before = fz[r, 8 * first_tile - 8:8 * first_tile, :] * (
                    next_z(sub, before, here) - before
                )
            else:
                here = source[r, 0:8, :]
                flux_before = jnp.zeros_like(here)
            for t in range(first_tile, end_tile):
                z = slice(8 * t, 8 * t + 8)
                above = source[r, 8 * t + 8:8 * t + 16, :] if t + 1 < tiles else jnp.zeros_like(here)
                flux_x = fx[r, z, :] * (source[r + 1, z, :] - here)
                flux_x -= fx[r - 1, z, :] * (here - source[r - 1, z, :])
                flux_y = fy[r, z, :] * (pltpu.roll(here, columns - 1, 1) - here)
                flux_y -= pltpu.roll(flux_y, 1, 1)
                flux = fz[r, z, :] * (next_z(sub, here, above) - here)
                flux_z = flux - jnp.where(sub == 0, pltpu.roll(flux_before, 1, 0), pltpu.roll(flux, 1, 0))
                value = here + STEP_SIZE * (flux_x + flux_y + flux_z)
                if last:
                    out[r - STEPS, 8 * t - 8:8 * t, :] = value
                else:
                    target[r, z, :] = value
                here, flux_before = above, flux
            return carry

        lax.fori_loop(step, rows - step, row_body, 0)
        source, target = target, source


def conduct_heat(groups, low, high, face_arrays):
    rows, tall, columns = face_arrays[0].shape
    parts = [p for _, group in groups for p in group]
    return pl.pallas_call(
        functools.partial(heat_kernel, [c for c, _ in groups]),
        out_shape=[jax.ShapeDtypeStruct((rows - 2 * STEPS, tall - 16, columns), jnp.float32)] * 2,
        in_specs=[VMEM] * (len(parts) + 5),
        out_specs=[VMEM] * 2,
        scratch_shapes=[pltpu.VMEM((rows, tall, columns), jnp.float32)] * 2,
        compiler_params=pltpu.CompilerParams(vmem_limit_bytes=VMEM_LIMIT),
        cost_estimate=cost(9.0),
    )(*parts, low, high, *face_arrays)


def second_kernel(holdp, fromp, holdm, fromm, token, outp, outm):
    outp[...] = holdp[...] + fromp[:2]
    outm[...] = holdm[...] + fromm[:2]


def ring_kernel(home, lastp, fromp, lastm, fromm, token, near, far):
    near[0] = home[0] + lastp[0] + fromm[2]
    far[0] = home[1] + lastp[1] + fromm[3]
    near[1] = home[2] + lastm[0] + fromp[2]
    far[1] = home[3] + lastm[1] + fromp[3]


def middle_kernel(near, got, token, out):
    out[...] = near[1] + got[1]


def volume_kernel(near, got, last, token, out):
    out[...] = near[0] + got[0] + last[...]


def small(body, outs, inputs, tokens=(), us=1.0):
    return pl.pallas_call(
        body,
        out_shape=[jax.ShapeDtypeStruct(o, jnp.float32) for o in outs],
        in_specs=[VMEM] * len(inputs) + [ANY] * len(tokens),
        out_specs=[VMEM] * len(outs),
        compiler_params=pltpu.CompilerParams(vmem_limit_bytes=VMEM_LIMIT),
        cost_estimate=cost(us),
    )(*inputs, *tokens)


class Chunk:
    def __init__(self, args, ranges, token):
        self.args, self.ranges = args, ranges
        theirs, self.started = backproject(*args, ranges, token)
        self.recv = shift_ang(theirs, dc=1)

    def first(self, token, us=6.0):
        *send, holdp, holdm, self.home = backproject(
            *self.args, self.ranges, token, self.recv, us=us
        )
        self.hold = holdp, holdm
        self.fromp = shift_ang(send[0], dx=1)
        self.fromm = shift_ang(send[1], dx=-1)
        return self.home

    def second(self, token):
        holdp, holdm = self.hold
        outs = small(
            second_kernel, [holdp.shape] * 2, [holdp, self.fromp, holdm, self.fromm], [token]
        )
        self.lastp = shift_ang(outs[0], dx=1)
        self.lastm = shift_ang(outs[1], dx=-1)
        return outs[0]

    def near_z(self, token, us=1.5):
        inputs = [self.home, self.lastp, self.fromp, self.lastm, self.fromm]
        shape = (2, *self.home.shape[1:])
        self.near, far = small(ring_kernel, [shape] * 2, inputs, [token], us=us)
        self.got = shift_ang(far, dz=1)
        return self.near

    def far_z(self, token):
        (out,) = small(middle_kernel, [self.home.shape[1:]], [self.near, self.got], [token])
        self.last = shift_ang(out, dz=2)
        return out

    def volume(self, token, us=1.0):
        parts = [self.near, self.got, self.last]
        return small(volume_kernel, [self.home.shape[1:]], parts, [token], us=us)[0]


def local(projections, band_weights, band_offsets, phase, contact, conductivity_table):
    ang = lax.axis_index("ang")
    core = ang & 1
    pos = jnp.stack([ang >> 3, (ang >> 1) & 3, core]).astype(jnp.int32)
    args = (pos, band_offsets, projections, band_weights)
    conduct, token = conductivities(conductivity_table, phase, contact, pos)
    outer = Chunk(args, CHUNKS[0], token)
    cond, token = widened(core, conduct, pos, us=SWAP_US)
    middle = Chunk(args, CHUNKS[1], pos)
    outer.first(middle.started, us=1.0)
    middle.first(outer.second(token))
    outer.near_z(pos, us=NEAR_US)
    token = outer.far_z(middle.second(pos))
    token = middle.near_z(token)
    outer_volume = outer.volume(token)
    token = middle.far_z(outer_volume)
    outer_rows, _ = widened(core, outer_volume, token)
    low, high = ends(cond, outer_rows)
    middle_volume = middle.volume(outer_volume, us=4.0)
    face_arrays = faces(cond, low, high, middle_volume)
    middle_rows, _ = widened(core, middle_volume, face_arrays[0])
    return conduct_heat(list(zip(CHUNKS, (outer_rows, middle_rows))), low, high, face_arrays)


def solution(mesh):
    in_specs = (
        P("ang", "gz", None),
        P("ang", None, None),
        P("ang", None),
        P("ang", "gz", None),
        P("ang", "gz", None),
        P(),
    )
    out_specs = (P("ang", "gz", None), P("ang", "gz", None))
    return jax.shard_map(local, mesh=mesh, in_specs=in_specs, out_specs=out_specs, check_vma=False)
```

```python
import functools
import jax
import jax.numpy as jnp
from jax import lax
from jax.experimental import pallas as pl
from jax.experimental.pallas import tpu as pltpu
from jax.sharding import PartitionSpec as P

STEPS = 4
STEP_SIZE = 0.15
CHUNKS = (((0, 16), (48, 16)), ((16, 32),))
TILE = 256
NEAR_US = 9.0
TOKEN = (8, 128)
SWAP_US = 40.0
ZL, X, C = 4, 4, 2
VMEM_LIMIT = 26 * 1024 * 1024


def shift_ang(value, dz=0, dx=0, dc=0):
    perm = []
    for z in range(ZL):
        for x in range(X):
            for c in range(C):
                src = (z * X + x) * C + c
                dst = ((z ^ dz) * X + (x + dx) % X) * C + (c ^ dc)
                perm.append((src, dst))
    return lax.ppermute(value, "ang", perm)


def shift_line(value, axis, step):
    count = lax.axis_size(axis)
    perm = [(i, i + step) for i in range(count) if 0 <= i + step < count]
    return lax.ppermute(value, axis, perm)


def gather(ranges, pos, offsets, proj, weights, wide, bands, flat, sems, core):
    angles, _, columns = proj.shape
    depth = wide.shape[1]
    copies = [
        pltpu.make_async_copy(weights.at[a], flat.at[:, a * 128:(a + 1) * 128], sems.at[a])
        for a in range(angles)
    ]
    for copy in copies:
        copy.start()
    wide[:, :, columns:] = jnp.zeros((angles, depth, 128), jnp.float32)
    for a in range(angles):
        at = 0
        for first, count in ranges:
            wide[a, at:at + count, :columns] = proj[a, first:first + count, :].astype(jnp.float32)
            at += count
    lane = lax.broadcasted_iota(jnp.int32, (depth, 128), 1)

    def row_body(row, carry):
        dx, dz, i = row >> 3, (row >> 1) & 3, row & 1
        owner = (
            (pos[0] ^ dz) * (X * C * 2)
            + ((pos[1] + dx) & (X - 1)) * (C * 2)
            + core * 2
            + i
        )
        for a in range(angles):
            off = offsets[a, owner]
            base = pl.multiple_of((off >> 7) << 7, 128)
            rem = off & 127
            low = wide[a, :, pl.ds(base, 128)]
            high = wide[a, :, pl.ds(pl.multiple_of(base + 128, 128), 128)]
            band = pltpu.roll(jnp.where(lane < rem, high, low), (128 - rem) & 127, 1)
            bands[pl.ds(pl.multiple_of(row * depth, depth), depth), a * 128:(a + 1) * 128] = (
                band.astype(jnp.bfloat16)
            )
        return carry

    lax.fori_loop(0, bands.shape[0] // depth, row_body, 0, unroll=4)
    for copy in copies:
        copy.wait()


def product(bands, flat, store):
    for n in range(0, flat.shape[0], TILE):
        out = lax.dot_general(
            bands[...],
            flat[n:n + TILE, :],
            (((1,), (1,)), ((), ())),
            preferred_element_type=jnp.float32,
        )
        store(out.reshape(4, 4, 2, bands.shape[0] // 32, TILE), slice(n, n + TILE))


def other_kernel(ranges, pos, offsets, proj, weights, token, out, done, wide, bands, flat, sems):
    done[...] = jnp.zeros(done.shape, jnp.float32)

    def store(value, cols):
        out[:, :, :, :, cols] = value

    gather(ranges, pos, offsets, proj, weights, wide, bands, flat, sems, 1 - pos[2])
    product(bands, flat, store)


def mine_kernel(
    ranges,
    pos,
    offsets,
    proj,
    weights,
    token,
    recv,
    sendp,
    sendm,
    holdp,
    holdm,
    home,
    wide,
    bands,
    flat,
    sems,
):
    def store(value, cols):
        value = value + recv[:, :, :, :, cols]
        sendp[:2, :, :, cols] = value[2, :2]
        sendp[2:, :, :, cols] = value[1, 2:]
        sendm[:2, :, :, cols] = value[2, 2:]
        sendm[2:, :, :, cols] = value[3, :2]
        holdp[:, :, :, cols] = value[1, :2]
        holdm[:, :, :, cols] = value[3, 2:]
        home[:, :, :, cols] = value[0]

    gather(ranges, pos, offsets, proj, weights, wide, bands, flat, sems, pos[2])
    product(bands, flat, store)


SMEM = pl.BlockSpec(memory_space=pltpu.SMEM)
VMEM = pl.BlockSpec(memory_space=pltpu.VMEM)
ANY = pl.BlockSpec(memory_space=pl.ANY)


def cost(us):
    return pl.CostEstimate(flops=int(us * 1.1e9), bytes_accessed=2**20, transcendentals=0)


def backproject(pos, offsets, proj, weights, ranges, token, recv=None, us=6.0):
    angles, _, columns = proj.shape
    wide_y, band = weights.shape[1:]
    depth = sum(count for _, count in ranges)
    full = lambda shape: pl.BlockSpec(shape, lambda n: (0,) * len(shape))
    params = dict(
        scratch_shapes=[
            pltpu.VMEM((angles, depth, columns + 128), jnp.float32),
            pltpu.VMEM((32 * depth, angles * band), jnp.bfloat16),
            pltpu.VMEM((wide_y, angles * band), jnp.bfloat16),
            pltpu.SemaphoreType.DMA((angles,)),
        ],
        grid=(1,),
        compiler_params=pltpu.CompilerParams(vmem_limit_bytes=VMEM_LIMIT),
        cost_estimate=cost(us),
    )
    specs = [SMEM, SMEM, full(proj.shape), ANY, ANY]
    f32 = lambda *shape: jax.ShapeDtypeStruct(shape, jnp.float32)
    if recv is None:
        shape = (4, 4, 2, depth, wide_y)
        return pl.pallas_call(
            functools.partial(other_kernel, ranges),
            out_shape=[f32(*shape), f32(*TOKEN)],
            in_specs=specs,
            out_specs=[full(shape), full(TOKEN)],
            **params,
        )(pos, offsets, proj, weights, token)
    shapes = [(n, 2, depth, wide_y) for n in (4, 4, 2, 2, 4)]
    return pl.pallas_call(
        functools.partial(mine_kernel, ranges),
        out_shape=[f32(*s) for s in shapes],
        in_specs=specs + [full(recv.shape)],
        out_specs=[full(s) for s in shapes],
        **params,
    )(pos, offsets, proj, weights, token, recv)


def conduct_kernel(table, phase, contact, token, out, done):
    done[...] = jnp.zeros(done.shape, jnp.float32)
    for r in range(phase.shape[0]):
        for z in range(0, phase.shape[1], 8):
            label = phase[r, z:z + 8, :]
            other = contact[r, z:z + 8, :]
            odd, upper = (other & 1) == 1, other >= 2
            odd_row, upper_row = (label & 1) == 1, label >= 2
            rows = [
                jnp.where(
                    upper,
                    jnp.where(odd, table[p, 3], table[p, 2]),
                    jnp.where(odd, table[p, 1], table[p, 0]),
                )
                for p in range(4)
            ]
            out[r, z:z + 8, :] = jnp.where(
                upper_row,
                jnp.where(odd_row, rows[3], rows[2]),
                jnp.where(odd_row, rows[1], rows[0]),
            )


def conductivities(table, phase, contact, token):
    return pl.pallas_call(
        conduct_kernel,
        out_shape=[jax.ShapeDtypeStruct(v, jnp.float32) for v in (phase.shape, TOKEN)],
        in_specs=[SMEM, VMEM, VMEM, ANY],
        out_specs=[VMEM, VMEM],
        cost_estimate=cost(2.0),
    )(table, phase, contact, token)


def swap_kernel(core, left, value, right, token, given):
    @pl.when(core[0] == 0)
    def _():
        given[:2] = value[...]
        given[2:] = right[...]

    @pl.when(core[0] != 0)
    def _():
        given[:2] = left[...]
        given[2:] = value[...]


def widened(core, value, token, us=1.0):
    left = shift_line(value, "ang", 2)
    right = shift_line(value, "ang", -2)
    _, depth, columns = value.shape
    given = pl.pallas_call(
        swap_kernel,
        out_shape=jax.ShapeDtypeStruct((4, depth, columns), jnp.float32),
        in_specs=[SMEM] + [VMEM] * 3 + [ANY],
        out_specs=VMEM,
        compiler_params=pltpu.CompilerParams(vmem_limit_bytes=VMEM_LIMIT),
        cost_estimate=cost(us),
    )(core.reshape(1), left, value, right, token)
    got = shift_ang(given, dc=1)
    return [left, got, value, right], given


def ends_kernel(*refs):
    top, bottom = refs[8:]
    for n in range(2):
        left, got, value, right = refs[4 * n:4 * n + 4]
        depth = value.shape[1]
        for out, z in ((top, slice(depth - 4, depth)), (bottom, slice(0, 4))):
            out[n, 0:2] = left[:, z]
            out[n, 2:4] = got[:2, z]
            out[n, 4:6] = value[:, z]
            out[n, 6:8] = got[2:, z]
            out[n, 8:10] = right[:, z]


def ends(cond, outer):
    shape = (2, 10, 4, outer[0].shape[2])
    top, bottom = small(ends_kernel, [shape] * 2, [*cond, *outer], us=3.0)
    return shift_line(top, "gz", 1), shift_line(bottom, "gz", -1)


def fill(scratch, groups, low, high, kind):
    rows, tall, columns = scratch.shape
    zeros = jnp.zeros((rows, 8, columns), jnp.float32)
    scratch[:, :8] = zeros
    scratch[:, tall - 8:] = zeros
    scratch[:, 4:8] = low[kind]
    scratch[:, tall - 8:tall - 4] = high[kind]
    for ranges, (left, got, value, right) in groups:
        at = 0
        for first, count in ranges:
            z, own = slice(8 + first, 8 + first + count), slice(at, at + count)
            scratch[0:2, z] = left[:, own]
            scratch[2:4, z] = got[:2, own]
            scratch[4:6, z] = value[:, own]
            scratch[6:8, z] = got[2:, own]
            scratch[8:10, z] = right[:, own]
            at += count


def face_of(a, b):
    total = a + b
    positive = total > 0.0
    return jnp.where(positive, 2.0 * a * b / jnp.where(positive, total, 1.0), 0.0)


def next_z(sub, here, above):
    return jnp.where(sub == 7, pltpu.roll(above, 7, 0), pltpu.roll(here, 7, 0))


def faces_kernel(left, got, value, right, low, high, token, fx, fy, fz, con):
    fill(con, [(((0, value.shape[1]),), (left, got, value, right))], low, high, 0)
    rows, tall, columns = con.shape
    tiles = tall // 8
    lane = lax.broadcasted_iota(jnp.int32, (8, columns), 1)
    sub = lax.broadcasted_iota(jnp.int32, (8, columns), 0)

    def face_body(r, carry):
        here = con[r, 0:8, :]
        for t in range(tiles):
            z = slice(8 * t, 8 * t + 8)
            above = con[r, 8 * t + 8:8 * t + 16, :] if t + 1 < tiles else jnp.zeros_like(here)
            along_y = pltpu.roll(here, columns - 1, 1)
            fy[r, z, :] = jnp.where(lane == columns - 1, 0.0, face_of(here, along_y))
            fz[r, z, :] = face_of(here, next_z(sub, here, above))
            fx[r, z, :] = face_of(here, con[jnp.minimum(r + 1, rows - 1), z, :])
            here = above
        return carry

    lax.fori_loop(0, rows, face_body, 0)


def faces(cond, low, high, token):
    _, depth, columns = cond[2].shape
    shape = (2 * STEPS + 2, depth + 16, columns)
    return pl.pallas_call(
        faces_kernel,
        out_shape=[jax.ShapeDtypeStruct(shape, jnp.float32)] * 3,
        in_specs=[VMEM] * 6 + [ANY],
        out_specs=[VMEM] * 3,
        scratch_shapes=[pltpu.VMEM(shape, jnp.float32)],
        compiler_params=pltpu.CompilerParams(vmem_limit_bytes=VMEM_LIMIT),
        cost_estimate=cost(6.0),
    )(*cond, low, high, token)


def heat_kernel(chunks, *refs):
    count = 4 * len(chunks)
    parts, (low, high, fx, fy, fz, volume, out, field, other) = refs[:count], refs[count:]
    groups = [(c, parts[4 * n:4 * n + 4]) for n, c in enumerate(chunks)]
    fill(field, groups, low, high, 1)
    volume[...] = field[STEPS:STEPS + volume.shape[0], 8:8 + volume.shape[1], :]
    rows, tall, columns = field.shape
    tiles = tall // 8
    sub = lax.broadcasted_iota(jnp.int32, (8, columns), 0)
    source, target = field, other
    for step in range(1, STEPS + 1):
        last = step == STEPS
        first_tile, end_tile = (1, tiles - 1) if last else (0, tiles)

        def row_body(r, carry, source=source, target=target, last=last, first_tile=first_tile, end_tile=end_tile):
            if first_tile:
                before = source[r, 8 * first_tile - 8:8 * first_tile, :]
                here = source[r, 8 * first_tile:8 * first_tile + 8, :]
                flux_before = fz[r, 8 * first_tile - 8:8 * first_tile, :] * (
                    next_z(sub, before, here) - before
                )
            else:
                here = source[r, 0:8, :]
                flux_before = jnp.zeros_like(here)
            for t in range(first_tile, end_tile):
                z = slice(8 * t, 8 * t + 8)
                above = source[r, 8 * t + 8:8 * t + 16, :] if t + 1 < tiles else jnp.zeros_like(here)
                flux_x = fx[r, z, :] * (source[r + 1, z, :] - here)
                flux_x -= fx[r - 1, z, :] * (here - source[r - 1, z, :])
                flux_y = fy[r, z, :] * (pltpu.roll(here, columns - 1, 1) - here)
                flux_y -= pltpu.roll(flux_y, 1, 1)
                flux = fz[r, z, :] * (next_z(sub, here, above) - here)
                flux_z = flux - jnp.where(sub == 0, pltpu.roll(flux_before, 1, 0), pltpu.roll(flux, 1, 0))
                value = here + STEP_SIZE * (flux_x + flux_y + flux_z)
                if last:
                    out[r - STEPS, 8 * t - 8:8 * t, :] = value
                else:
                    target[r, z, :] = value
                here, flux_before = above, flux
            return carry

        lax.fori_loop(step, rows - step, row_body, 0)
        source, target = target, source


def conduct_heat(groups, low, high, face_arrays):
    rows, tall, columns = face_arrays[0].shape
    parts = [p for _, group in groups for p in group]
    return pl.pallas_call(
        functools.partial(heat_kernel, [c for c, _ in groups]),
        out_shape=[jax.ShapeDtypeStruct((rows - 2 * STEPS, tall - 16, columns), jnp.float32)] * 2,
        in_specs=[VMEM] * (len(parts) + 5),
        out_specs=[VMEM] * 2,
        scratch_shapes=[pltpu.VMEM((rows, tall, columns), jnp.float32)] * 2,
        compiler_params=pltpu.CompilerParams(vmem_limit_bytes=VMEM_LIMIT),
        cost_estimate=cost(9.0),
    )(*parts, low, high, *face_arrays)


def second_kernel(holdp, fromp, holdm, fromm, token, outp, outm):
    outp[...] = holdp[...] + fromp[:2]
    outm[...] = holdm[...] + fromm[:2]


def ring_kernel(home, lastp, fromp, lastm, fromm, token, near, far):
    near[0] = home[0] + lastp[0] + fromm[2]
    far[0] = home[1] + lastp[1] + fromm[3]
    near[1] = home[2] + lastm[0] + fromp[2]
    far[1] = home[3] + lastm[1] + fromp[3]


def middle_kernel(near, got, token, out):
    out[...] = near[1] + got[1]


def volume_kernel(near, got, last, token, out):
    out[...] = near[0] + got[0] + last[...]


def small(body, outs, inputs, tokens=(), us=1.0):
    return pl.pallas_call(
        body,
        out_shape=[jax.ShapeDtypeStruct(o, jnp.float32) for o in outs],
        in_specs=[VMEM] * len(inputs) + [ANY] * len(tokens),
        out_specs=[VMEM] * len(outs),
        compiler_params=pltpu.CompilerParams(vmem_limit_bytes=VMEM_LIMIT),
        cost_estimate=cost(us),
    )(*inputs, *tokens)


class Chunk:
    def __init__(self, args, ranges, token):
        self.args, self.ranges = args, ranges
        theirs, self.started = backproject(*args, ranges, token)
        self.recv = shift_ang(theirs, dc=1)

    def first(self, token, us=6.0):
        *send, holdp, holdm, self.home = backproject(
            *self.args, self.ranges, token, self.recv, us=us
        )
        self.hold = holdp, holdm
        self.fromp = shift_ang(send[0], dx=1)
        self.fromm = shift_ang(send[1], dx=-1)
        return self.home

    def second(self, token):
        holdp, holdm = self.hold
        outs = small(
            second_kernel, [holdp.shape] * 2, [holdp, self.fromp, holdm, self.fromm], [token]
        )
        self.lastp = shift_ang(outs[0], dx=1)
        self.lastm = shift_ang(outs[1], dx=-1)
        return outs[0]

    def near_z(self, token, us=1.5):
        inputs = [self.home, self.lastp, self.fromp, self.lastm, self.fromm]
        shape = (2, *self.home.shape[1:])
        self.near, far = small(ring_kernel, [shape] * 2, inputs, [token], us=us)
        self.got = shift_ang(far, dz=1)
        return self.near

    def far_z(self, token):
        (out,) = small(middle_kernel, [self.home.shape[1:]], [self.near, self.got], [token])
        self.last = shift_ang(out, dz=2)
        return out

    def volume(self, token, us=1.0):
        parts = [self.near, self.got, self.last]
        return small(volume_kernel, [self.home.shape[1:]], parts, [token], us=us)[0]


def local(projections, band_weights, band_offsets, phase, contact, conductivity_table):
    ang = lax.axis_index("ang")
    core = ang & 1
    pos = jnp.stack([ang >> 3, (ang >> 1) & 3, core]).astype(jnp.int32)
    args = (pos, band_offsets, projections, band_weights)
    conduct, token = conductivities(conductivity_table, phase, contact, pos)
    outer = Chunk(args, CHUNKS[0], token)
    cond, token = widened(core, conduct, pos, us=SWAP_US)
    middle = Chunk(args, CHUNKS[1], pos)
    outer.first(middle.started, us=1.0)
    middle.first(outer.second(token))
    outer.near_z(pos, us=NEAR_US)
    token = outer.far_z(middle.second(pos))
    token = middle.near_z(token)
    outer_volume = outer.volume(token)
    token = middle.far_z(outer_volume)
    outer_rows, _ = widened(core, outer_volume, pos)
    low, high = ends(cond, outer_rows)
    middle_volume = middle.volume(outer_volume, us=4.0)
    face_arrays = faces(cond, low, high, middle_volume)
    middle_rows, _ = widened(core, middle_volume, face_arrays[0])
    return conduct_heat(list(zip(CHUNKS, (outer_rows, middle_rows))), low, high, face_arrays)


def solution(mesh):
    in_specs = (
        P("ang", "gz", None),
        P("ang", None, None),
        P("ang", None),
        P("ang", "gz", None),
        P("ang", "gz", None),
        P(),
    )
    out_specs = (P("ang", "gz", None), P("ang", "gz", None))
    return jax.shard_map(local, mesh=mesh, in_specs=in_specs, out_specs=out_specs, check_vma=False)
```

```python
import functools
import jax
import jax.numpy as jnp
from jax import lax
from jax.experimental import pallas as pl
from jax.experimental.pallas import tpu as pltpu
from jax.sharding import PartitionSpec as P

STEPS = 4
STEP_SIZE = 0.15
CHUNKS = (((0, 16), (48, 16)), ((16, 32),))
TILE = 256
NEAR_US = 9.0
TOKEN = (8, 128)
SWAP_US = 40.0
ZL, X, C = 4, 4, 2
VMEM_LIMIT = 26 * 1024 * 1024


def shift_ang(value, dz=0, dx=0, dc=0):
    perm = []
    for z in range(ZL):
        for x in range(X):
            for c in range(C):
                src = (z * X + x) * C + c
                dst = ((z ^ dz) * X + (x + dx) % X) * C + (c ^ dc)
                perm.append((src, dst))
    return lax.ppermute(value, "ang", perm)


def shift_line(value, axis, step):
    count = lax.axis_size(axis)
    perm = [(i, i + step) for i in range(count) if 0 <= i + step < count]
    return lax.ppermute(value, axis, perm)


def gather(ranges, pos, offsets, proj, weights, wide, bands, flat, sems, core):
    angles, _, columns = proj.shape
    depth = wide.shape[1]
    copies = [
        pltpu.make_async_copy(weights.at[a], flat.at[:, a * 128:(a + 1) * 128], sems.at[a])
        for a in range(angles)
    ]
    for copy in copies:
        copy.start()
    wide[:, :, columns:] = jnp.zeros((angles, depth, 128), jnp.float32)
    for a in range(angles):
        at = 0
        for first, count in ranges:
            wide[a, at:at + count, :columns] = proj[a, first:first + count, :].astype(jnp.float32)
            at += count
    lane = lax.broadcasted_iota(jnp.int32, (depth, 128), 1)

    def row_body(row, carry):
        dx, dz, i = row >> 3, (row >> 1) & 3, row & 1
        owner = (
            (pos[0] ^ dz) * (X * C * 2)
            + ((pos[1] + dx) & (X - 1)) * (C * 2)
            + core * 2
            + i
        )
        for a in range(angles):
            off = offsets[a, owner]
            base = pl.multiple_of((off >> 7) << 7, 128)
            rem = off & 127
            low = wide[a, :, pl.ds(base, 128)]
            high = wide[a, :, pl.ds(pl.multiple_of(base + 128, 128), 128)]
            band = pltpu.roll(jnp.where(lane < rem, high, low), (128 - rem) & 127, 1)
            bands[pl.ds(pl.multiple_of(row * depth, depth), depth), a * 128:(a + 1) * 128] = (
                band.astype(jnp.bfloat16)
            )
        return carry

    lax.fori_loop(0, bands.shape[0] // depth, row_body, 0, unroll=4)
    for copy in copies:
        copy.wait()


def product(bands, flat, store):
    for n in range(0, flat.shape[0], TILE):
        out = lax.dot_general(
            bands[...],
            flat[n:n + TILE, :],
            (((1,), (1,)), ((), ())),
            preferred_element_type=jnp.float32,
        )
        store(out.reshape(4, 4, 2, bands.shape[0] // 32, TILE), slice(n, n + TILE))


def other_kernel(ranges, pos, offsets, proj, weights, token, out, done, wide, bands, flat, sems):
    done[...] = jnp.zeros(done.shape, jnp.float32)

    def store(value, cols):
        out[:, :, :, :, cols] = value

    gather(ranges, pos, offsets, proj, weights, wide, bands, flat, sems, 1 - pos[2])
    product(bands, flat, store)


def mine_kernel(
    ranges,
    pos,
    offsets,
    proj,
    weights,
    token,
    recv,
    sendp,
    sendm,
    holdp,
    holdm,
    home,
    wide,
    bands,
    flat,
    sems,
):
    def store(value, cols):
        value = value + recv[:, :, :, :, cols]
        sendp[:2, :, :, cols] = value[2, :2]
        sendp[2:, :, :, cols] = value[1, 2:]
        sendm[:2, :, :, cols] = value[2, 2:]
        sendm[2:, :, :, cols] = value[3, :2]
        holdp[:, :, :, cols] = value[1, :2]
        holdm[:, :, :, cols] = value[3, 2:]
        home[:, :, :, cols] = value[0]

    gather(ranges, pos, offsets, proj, weights, wide, bands, flat, sems, pos[2])
    product(bands, flat, store)


SMEM = pl.BlockSpec(memory_space=pltpu.SMEM)
VMEM = pl.BlockSpec(memory_space=pltpu.VMEM)
ANY = pl.BlockSpec(memory_space=pl.ANY)


def cost(us):
    return pl.CostEstimate(flops=int(us * 1.1e9), bytes_accessed=2**20, transcendentals=0)


def backproject(pos, offsets, proj, weights, ranges, token, recv=None, us=6.0):
    angles, _, columns = proj.shape
    wide_y, band = weights.shape[1:]
    depth = sum(count for _, count in ranges)
    full = lambda shape: pl.BlockSpec(shape, lambda n: (0,) * len(shape))
    params = dict(
        scratch_shapes=[
            pltpu.VMEM((angles, depth, columns + 128), jnp.float32),
            pltpu.VMEM((32 * depth, angles * band), jnp.bfloat16),
            pltpu.VMEM((wide_y, angles * band), jnp.bfloat16),
            pltpu.SemaphoreType.DMA((angles,)),
        ],
        grid=(1,),
        compiler_params=pltpu.CompilerParams(vmem_limit_bytes=VMEM_LIMIT),
        cost_estimate=cost(us),
    )
    specs = [SMEM, SMEM, full(proj.shape), ANY, ANY]
    f32 = lambda *shape: jax.ShapeDtypeStruct(shape, jnp.float32)
    if recv is None:
        shape = (4, 4, 2, depth, wide_y)
        return pl.pallas_call(
            functools.partial(other_kernel, ranges),
            out_shape=[f32(*shape), f32(*TOKEN)],
            in_specs=specs,
            out_specs=[full(shape), full(TOKEN)],
            **params,
        )(pos, offsets, proj, weights, token)
    shapes = [(n, 2, depth, wide_y) for n in (4, 4, 2, 2, 4)]
    return pl.pallas_call(
        functools.partial(mine_kernel, ranges),
        out_shape=[f32(*s) for s in shapes],
        in_specs=specs + [full(recv.shape)],
        out_specs=[full(s) for s in shapes],
        **params,
    )(pos, offsets, proj, weights, token, recv)


def conduct_kernel(table, phase, contact, token, out, done):
    done[...] = jnp.zeros(done.shape, jnp.float32)
    for r in range(phase.shape[0]):
        for z in range(0, phase.shape[1], 8):
            label = phase[r, z:z + 8, :]
            other = contact[r, z:z + 8, :]
            odd, upper = (other & 1) == 1, other >= 2
            odd_row, upper_row = (label & 1) == 1, label >= 2
            rows = [
                jnp.where(
                    upper,
                    jnp.where(odd, table[p, 3], table[p, 2]),
                    jnp.where(odd, table[p, 1], table[p, 0]),
                )
                for p in range(4)
            ]
            out[r, z:z + 8, :] = jnp.where(
                upper_row,
                jnp.where(odd_row, rows[3], rows[2]),
                jnp.where(odd_row, rows[1], rows[0]),
            )


def conductivities(table, phase, contact, token):
    return pl.pallas_call(
        conduct_kernel,
        out_shape=[jax.ShapeDtypeStruct(v, jnp.float32) for v in (phase.shape, TOKEN)],
        in_specs=[SMEM, VMEM, VMEM, ANY],
        out_specs=[VMEM, VMEM],
        cost_estimate=cost(2.0),
    )(table, phase, contact, token)


def swap_kernel(core, left, value, right, token, given):
    @pl.when(core[0] == 0)
    def _():
        given[:2] = value[...]
        given[2:] = right[...]

    @pl.when(core[0] != 0)
    def _():
        given[:2] = left[...]
        given[2:] = value[...]


def widened(core, value, token, us=1.0):
    left = shift_line(value, "ang", 2)
    right = shift_line(value, "ang", -2)
    _, depth, columns = value.shape
    given = pl.pallas_call(
        swap_kernel,
        out_shape=jax.ShapeDtypeStruct((4, depth, columns), jnp.float32),
        in_specs=[SMEM] + [VMEM] * 3 + [ANY],
        out_specs=VMEM,
        compiler_params=pltpu.CompilerParams(vmem_limit_bytes=VMEM_LIMIT),
        cost_estimate=cost(us),
    )(core.reshape(1), left, value, right, token)
    got = shift_ang(given, dc=1)
    return [left, got, value, right], given


def ends_kernel(*refs):
    top, bottom = refs[8:]
    for n in range(2):
        left, got, value, right = refs[4 * n:4 * n + 4]
        depth = value.shape[1]
        for out, z in ((top, slice(depth - 4, depth)), (bottom, slice(0, 4))):
            out[n, 0:2] = left[:, z]
            out[n, 2:4] = got[:2, z]
            out[n, 4:6] = value[:, z]
            out[n, 6:8] = got[2:, z]
            out[n, 8:10] = right[:, z]


def ends(cond, outer):
    shape = (2, 10, 4, outer[0].shape[2])
    top, bottom = small(ends_kernel, [shape] * 2, [*cond, *outer], us=3.0)
    return shift_line(top, "gz", 1), shift_line(bottom, "gz", -1)


def fill(scratch, groups, low, high, kind):
    rows, tall, columns = scratch.shape
    zeros = jnp.zeros((rows, 8, columns), jnp.float32)
    scratch[:, :8] = zeros
    scratch[:, tall - 8:] = zeros
    scratch[:, 4:8] = low[kind]
    scratch[:, tall - 8:tall - 4] = high[kind]
    for ranges, (left, got, value, right) in groups:
        at = 0
        for first, count in ranges:
            z, own = slice(8 + first, 8 + first + count), slice(at, at + count)
            scratch[0:2, z] = left[:, own]
            scratch[2:4, z] = got[:2, own]
            scratch[4:6, z] = value[:, own]
            scratch[6:8, z] = got[2:, own]
            scratch[8:10, z] = right[:, own]
            at += count


def face_of(a, b):
    total = a + b
    positive = total > 0.0
    return jnp.where(positive, 2.0 * a * b / jnp.where(positive, total, 1.0), 0.0)


def next_z(sub, here, above):
    return jnp.where(sub == 7, pltpu.roll(above, 7, 0), pltpu.roll(here, 7, 0))


def faces_kernel(left, got, value, right, low, high, token, fx, fy, fz, con):
    fill(con, [(((0, value.shape[1]),), (left, got, value, right))], low, high, 0)
    rows, tall, columns = con.shape
    tiles = tall // 8
    lane = lax.broadcasted_iota(jnp.int32, (8, columns), 1)
    sub = lax.broadcasted_iota(jnp.int32, (8, columns), 0)

    def face_body(r, carry):
        here = con[r, 0:8, :]
        for t in range(tiles):
            z = slice(8 * t, 8 * t + 8)
            above = con[r, 8 * t + 8:8 * t + 16, :] if t + 1 < tiles else jnp.zeros_like(here)
            along_y = pltpu.roll(here, columns - 1, 1)
            fy[r, z, :] = jnp.where(lane == columns - 1, 0.0, face_of(here, along_y))
            fz[r, z, :] = face_of(here, next_z(sub, here, above))
            fx[r, z, :] = face_of(here, con[jnp.minimum(r + 1, rows - 1), z, :])
            here = above
        return carry

    lax.fori_loop(0, rows, face_body, 0)


def faces(cond, low, high, token):
    _, depth, columns = cond[2].shape
    shape = (2 * STEPS + 2, depth + 16, columns)
    return pl.pallas_call(
        faces_kernel,
        out_shape=[jax.ShapeDtypeStruct(shape, jnp.float32)] * 3,
        in_specs=[VMEM] * 6 + [ANY],
        out_specs=[VMEM] * 3,
        scratch_shapes=[pltpu.VMEM(shape, jnp.float32)],
        compiler_params=pltpu.CompilerParams(vmem_limit_bytes=VMEM_LIMIT),
        cost_estimate=cost(6.0),
    )(*cond, low, high, token)


def heat_kernel(chunks, *refs):
    count = 4 * len(chunks)
    parts, (low, high, fx, fy, fz, volume, out, field, other) = refs[:count], refs[count:]
    groups = [(c, parts[4 * n:4 * n + 4]) for n, c in enumerate(chunks)]
    fill(field, groups, low, high, 1)
    volume[...] = field[STEPS:STEPS + volume.shape[0], 8:8 + volume.shape[1], :]
    rows, tall, columns = field.shape
    tiles = tall // 8
    sub = lax.broadcasted_iota(jnp.int32, (8, columns), 0)
    source, target = field, other
    for step in range(1, STEPS + 1):
        last = step == STEPS
        first_tile, end_tile = (1, tiles - 1) if last else (0, tiles)

        def row_body(r, carry, source=source, target=target, last=last, first_tile=first_tile, end_tile=end_tile):
            if first_tile:
                before = source[r, 8 * first_tile - 8:8 * first_tile, :]
                here = source[r, 8 * first_tile:8 * first_tile + 8, :]
                flux_before = fz[r, 8 * first_tile - 8:8 * first_tile, :] * (
                    next_z(sub, before, here) - before
                )
            else:
                here = source[r, 0:8, :]
                flux_before = jnp.zeros_like(here)
            for t in range(first_tile, end_tile):
                z = slice(8 * t, 8 * t + 8)
                above = source[r, 8 * t + 8:8 * t + 16, :] if t + 1 < tiles else jnp.zeros_like(here)
                flux_x = fx[r, z, :] * (source[r + 1, z, :] - here)
                flux_x -= fx[r - 1, z, :] * (here - source[r - 1, z, :])
                flux_y = fy[r, z, :] * (pltpu.roll(here, columns - 1, 1) - here)
                flux_y -= pltpu.roll(flux_y, 1, 1)
                flux = fz[r, z, :] * (next_z(sub, here, above) - here)
                flux_z = flux - jnp.where(sub == 0, pltpu.roll(flux_before, 1, 0), pltpu.roll(flux, 1, 0))
                value = here + STEP_SIZE * (flux_x + flux_y + flux_z)
                if last:
                    out[r - STEPS, 8 * t - 8:8 * t, :] = value
                else:
                    target[r, z, :] = value
                here, flux_before = above, flux
            return carry

        lax.fori_loop(step, rows - step, row_body, 0)
        source, target = target, source


def conduct_heat(groups, low, high, face_arrays):
    rows, tall, columns = face_arrays[0].shape
    parts = [p for _, group in groups for p in group]
    return pl.pallas_call(
        functools.partial(heat_kernel, [c for c, _ in groups]),
        out_shape=[jax.ShapeDtypeStruct((rows - 2 * STEPS, tall - 16, columns), jnp.float32)] * 2,
        in_specs=[VMEM] * (len(parts) + 5),
        out_specs=[VMEM] * 2,
        scratch_shapes=[pltpu.VMEM((rows, tall, columns), jnp.float32)] * 2,
        compiler_params=pltpu.CompilerParams(vmem_limit_bytes=VMEM_LIMIT),
        cost_estimate=cost(9.0),
    )(*parts, low, high, *face_arrays)


def second_kernel(holdp, fromp, holdm, fromm, token, outp, outm):
    outp[...] = holdp[...] + fromp[:2]
    outm[...] = holdm[...] + fromm[:2]


def ring_kernel(home, lastp, fromp, lastm, fromm, token, near, far):
    near[0] = home[0] + lastp[0] + fromm[2]
    far[0] = home[1] + lastp[1] + fromm[3]
    near[1] = home[2] + lastm[0] + fromp[2]
    far[1] = home[3] + lastm[1] + fromp[3]


def middle_kernel(near, got, token, out):
    out[...] = near[1] + got[1]


def volume_kernel(near, got, last, token, out):
    out[...] = near[0] + got[0] + last[...]


def small(body, outs, inputs, tokens=(), us=1.0):
    return pl.pallas_call(
        body,
        out_shape=[jax.ShapeDtypeStruct(o, jnp.float32) for o in outs],
        in_specs=[VMEM] * len(inputs) + [ANY] * len(tokens),
        out_specs=[VMEM] * len(outs),
        compiler_params=pltpu.CompilerParams(vmem_limit_bytes=VMEM_LIMIT),
        cost_estimate=cost(us),
    )(*inputs, *tokens)


class Chunk:
    def __init__(self, args, ranges, token):
        self.args, self.ranges = args, ranges
        theirs, self.started = backproject(*args, ranges, token)
        self.recv = shift_ang(theirs, dc=1)

    def first(self, token, us=6.0):
        *send, holdp, holdm, self.home = backproject(
            *self.args, self.ranges, token, self.recv, us=us
        )
        self.hold = holdp, holdm
        self.fromp = shift_ang(send[0], dx=1)
        self.fromm = shift_ang(send[1], dx=-1)
        return self.home

    def second(self, token, us=1.0):
        holdp, holdm = self.hold
        outs = small(
            second_kernel, [holdp.shape] * 2, [holdp, self.fromp, holdm, self.fromm], [token], us=us
        )
        self.lastp = shift_ang(outs[0], dx=1)
        self.lastm = shift_ang(outs[1], dx=-1)
        return outs[0]

    def near_z(self, token, us=1.5):
        inputs = [self.home, self.lastp, self.fromp, self.lastm, self.fromm]
        shape = (2, *self.home.shape[1:])
        self.near, far = small(ring_kernel, [shape] * 2, inputs, [token], us=us)
        self.got = shift_ang(far, dz=1)
        return self.near

    def far_z(self, token):
        (out,) = small(middle_kernel, [self.home.shape[1:]], [self.near, self.got], [token])
        self.last = shift_ang(out, dz=2)
        return out

    def volume(self, token, us=1.0):
        parts = [self.near, self.got, self.last]
        return small(volume_kernel, [self.home.shape[1:]], parts, [token], us=us)[0]


def local(projections, band_weights, band_offsets, phase, contact, conductivity_table):
    ang = lax.axis_index("ang")
    core = ang & 1
    pos = jnp.stack([ang >> 3, (ang >> 1) & 3, core]).astype(jnp.int32)
    args = (pos, band_offsets, projections, band_weights)
    conduct, token = conductivities(conductivity_table, phase, contact, pos)
    outer = Chunk(args, CHUNKS[0], token)
    cond, token = widened(core, conduct, pos, us=SWAP_US)
    middle = Chunk(args, CHUNKS[1], pos)
    outer.first(middle.started, us=1.0)
    middle.first(outer.second(token))
    outer.near_z(pos, us=NEAR_US)
    token = middle.second(outer.far_z(pos), us=4.0)
    outer_volume = outer.volume(token)
    middle.near_z(outer_volume, us=4.0)
    token = middle.far_z(outer_volume)
    outer_rows, _ = widened(core, outer_volume, token)
    low, high = ends(cond, outer_rows)
    middle_volume = middle.volume(outer_volume, us=4.0)
    face_arrays = faces(cond, low, high, middle_volume)
    middle_rows, _ = widened(core, middle_volume, face_arrays[0])
    return conduct_heat(list(zip(CHUNKS, (outer_rows, middle_rows))), low, high, face_arrays)


def solution(mesh):
    in_specs = (
        P("ang", "gz", None),
        P("ang", None, None),
        P("ang", None),
        P("ang", "gz", None),
        P("ang", "gz", None),
        P(),
    )
    out_specs = (P("ang", "gz", None), P("ang", "gz", None))
    return jax.shard_map(local, mesh=mesh, in_specs=in_specs, out_specs=out_specs, check_vma=False)
```
